512 devices in a mesh: tok: 32 (over y_hi, x, core), feat: 16 (over y_lo, z).
Axes of the slice: x: 4, y: 8 (y_hi: 4, y_lo: 2; y = y_hi * 2 + y_lo), z: 8, core: 2. Of those that a mesh axis runs over, the one named last changes fastest.
Arguments:
- entering: bfloat16 [2560, 32768], P('feat', 'tok'), may hold values from -210 to 210
- leaving: bfloat16 [2560, 32768], P('feat', 'tok'), may hold values from -280 to 280
Outputs:
- transform: float32 [2560, 2560], P('feat', 'tok')
The draws below stay inside these ranges and needn't reach their ends.
All inputs are finite; a program needn't handle non-finite values.
Results may differ from the reference program's by a relative error of at most 0.00052.
Values may be sent and summed in bfloat16 or wider, within the bound.
No kernel may reach another device: no remote copies, remote signals or barrier semaphores. Data moves between devices by JAX's collectives and lax.ppermute only.
A program may use at most 64 MiB of HBM per device.

```python
import math
import jax
import jax.numpy as jnp
from jax import lax

D = 2560
ITERS = 2
TOKENS = 32768


def common_pair(key):
    folded = jax.random.fold_in(key, 11)
    subkeys = jax.random.split(folded, 5)
    position = jnp.arange(TOKENS, dtype=jnp.float32)[:, None] / TOKENS
    feature_pos = jnp.arange(D, dtype=jnp.float32)[None, :] / D
    row_scale = jnp.exp(jax.random.uniform(subkeys[0], (TOKENS, 1), jnp.float32, 0.0, math.log(10.0)))
    row_scale = row_scale * jnp.exp(0.5 * math.log(10.0) * position)
    col_scale = jnp.exp(jax.random.uniform(subkeys[1], (1, D), jnp.float32, 0.0, math.log(10.0)))
    col_scale = col_scale * jnp.exp(0.5 * math.log(3.0) * feature_pos)
    residue = jax.random.normal(subkeys[4], (TOKENS, D), jnp.float32)
    pattern = jnp.clip(jax.random.normal(subkeys[2], (TOKENS, D), jnp.float32), -6.0, 6.0)
    residue = jnp.clip(residue, -6.0, 6.0)
    combined = row_scale * col_scale / 16.0
    entering = pattern * combined
    leaving = 0.8 * entering + 0.5 * residue * combined
    return (entering.T, leaving.T)


def draw_entering(key, part):
    return common_pair(key)[0].astype(jnp.bfloat16)


def draw_leaving(key, part):
    return common_pair(key)[1].astype(jnp.bfloat16)


def setup_inputs(seed: int = 0) -> dict:
    seeds = jax.random.split(jax.random.key(seed), 3)
    return {
        "entering": draw_entering(jax.random.fold_in(seeds[2], 71), 0),
        "leaving": draw_leaving(jax.random.fold_in(seeds[2], 71), 0),
    }


ridge_share = 0.2


def reference(entering, leaving):
    gram = jnp.dot(entering, entering.T, preferred_element_type=jnp.float32)
    cross = jnp.dot(entering, leaving.T, preferred_element_type=jnp.float32)
    energy = jnp.sum(jnp.square(entering.astype(jnp.float32)))
    ridge_term = ridge_share * energy / (TOKENS * D)
    upper_bound = jnp.max(jnp.sum(jnp.abs(gram), axis=1)) / TOKENS + ridge_term
    center = (upper_bound + ridge_term) / 2.0
    half_span = (upper_bound - ridge_term) / 2.0
    target = cross / TOKENS
    transform = target / center
    update = transform
    ratio_now = half_span / center
    for sweep in range(ITERS):
        iterate_half = lax.optimization_barrier(transform.astype(jnp.bfloat16))
        widened = iterate_half.astype(jnp.float32)
        applied = jnp.dot(gram, widened, precision=lax.Precision.HIGHEST)
        residual_now = target - (applied / TOKENS + ridge_term * widened)
        ratio_next = 1.0 / (2.0 * center / half_span - ratio_now)
        update = ratio_next * ratio_now * update + (2.0 * ratio_next / half_span) * residual_now
        transform = transform + update
        ratio_now = ratio_next
    return transform
```

```python
import jax
import jax.numpy as jnp
import numpy as np
from jax import lax
from jax.sharding import Mesh, PartitionSpec as P

ITERS = 2
ridge_share = 0.2
TOK = ("yh", "x", "c")
FEAT = ("yl", "z")
ALL = TOK + FEAT
SIZES = (4, 4, 2, 2, 8)


def shift(array, axis, size, step):
    return lax.ppermute(array, axis, [(i, (i + step) % size) for i in range(size)])


def spread(array, axes, count):
    return lax.all_to_all(
        jnp.broadcast_to(array[None], (count,) + array.shape), axes, 0, 0
    )


def tile_moves():
    moves = []
    for yh in range(4):
        for x in range(4):
            for c in range(2):
                for yl in range(2):
                    for z in range(8):
                        other_yl, half = yh // 2, yh % 2
                        source = (((yh * 4 + x) * 2 + c) * 2 + yl) * 8 + z
                        to_z = (z + 4 * c + x) % 8
                        to_yh, to_x = other_yl * 2 + z // 4, z % 4
                        target = (((to_yh * 4 + to_x) * 2 + half) * 2 + yl) * 8 + to_z
                        moves.append((source, target))
    return moves


def body(entering, leaving):
    yl = lax.axis_index("yl")
    z = lax.axis_index("z")
    rows = entering.shape[0]
    quarter = rows // 4
    half_cols = rows // 2
    token_total = entering.shape[1] * 32
    order_all = rows * 16
    low = yl == 0

    pair = jnp.concatenate([entering, leaving], 0)
    other = shift(pair, "yl", 2, 1)
    first = jnp.where(low, pair, other)
    second = jnp.where(low, other, pair)
    columns = jnp.concatenate([first[:rows], second[:rows], first[rows:], second[rows:]], 0)

    blocks = {0: entering}
    up = down = entering
    for step in range(1, 5):
        down = shift(down, "z", 8, -1)
        blocks[step] = down
        if step < 4:
            up = shift(up, "z", 8, 1)
            blocks[8 - step] = up

    pieces = [
        lax.dot_general(
            blocks[s], columns, (((1,), (1,)), ((), ())), preferred_element_type=jnp.float32
        )
        for s in range(8)
    ]
    partial = jnp.stack(pieces).reshape(2, 4, rows, 4 * rows)
    partial = jnp.sum(lax.all_to_all(partial, "c", 0, 0), 0)
    partial = jnp.sum(lax.all_to_all(partial, "x", 0, 0), 0)
    packed = jnp.stack(
        [
            jnp.concatenate(
                [partial[quarter * q : quarter * (q + 1), : 2 * rows]]
                + [
                    partial[
                        quarter * r : quarter * (r + 1),
                        2 * rows + half_cols * q : 2 * rows + half_cols * (q + 1),
                    ]
                    for r in range(4)
                ],
                1,
            )
            for q in range(4)
        ]
    )
    own = jnp.sum(lax.all_to_all(packed, "yh", 0, 0), 0)
    gram_own = own[:, : 2 * rows]
    cross_own = lax.ppermute(own[:, 2 * rows :], ALL, tile_moves())
    cross_tile = jnp.concatenate(
        [cross_own[:, half_cols * r : half_cols * (r + 1)] for r in range(4)], 0
    )

    gram_swap = shift(gram_own, "yl", 2, 1)
    gram_swap = jnp.concatenate([gram_swap[:, rows:], gram_swap[:, :rows]], 1)
    slot = lax.broadcasted_iota(jnp.int32, gram_own.shape, 1) // rows
    gram_part = jnp.where(slot == yl, gram_own, gram_swap)
    gram_part = spread(gram_part, "yh", 4).reshape(rows, 2 * rows)
    gram_part = spread(gram_part, "x", 4)
    gram = spread(gram_part, "c", 2).reshape(8, rows, 2 * rows)

    sums = jnp.sum(jnp.abs(gram), (0, 1))
    row_peak = jnp.max(sums[:rows] + sums[rows:])
    at_row = lax.broadcasted_iota(jnp.int32, (rows, 2 * rows), 0)
    at_col = lax.broadcasted_iota(jnp.int32, (rows, 2 * rows), 1)
    trace = jnp.sum(jnp.where(at_col == at_row + rows * yl, gram[0], 0.0))
    lane = lax.broadcasted_iota(jnp.int32, (1, 128), 1)
    scalars = spread(jnp.where(lane == 0, row_peak, trace), FEAT, 16)
    peak_all = jnp.max(scalars[:, 0, 0])
    energy = jnp.sum(scalars[:, 0, 1])

    ridge_term = ridge_share * energy / (token_total * order_all)
    upper_bound = peak_all / token_total + ridge_term
    center = (upper_bound + ridge_term) / 2.0
    half_span = (upper_bound - ridge_term) / 2.0

    gram_flat = gram.reshape(8 * rows, 2 * rows)
    gram_hi = gram_flat.astype(jnp.bfloat16)
    gram_lo = (gram_flat - gram_hi.astype(jnp.float32)).astype(jnp.bfloat16)
    gram_both = jnp.concatenate([gram_hi, gram_lo], 1)

    target = cross_tile / token_total
    transform = target / center
    update = transform
    ratio_now = half_span / center
    for sweep in range(ITERS):
        iterate_half = transform.astype(jnp.bfloat16)
        full = spread(iterate_half, FEAT, 16).reshape(2, 8, rows, half_cols)
        full = jnp.concatenate([full, full], 1)
        full = lax.dynamic_slice_in_dim(full, z, 8, 1).reshape(2, 8 * rows, half_cols)
        products = [
            lax.dot_general(
                gram_both, full[k], (((0,), (0,)), ((), ())), preferred_element_type=jnp.float32
            )
            for k in range(2)
        ]
        applied = (
            products[0][:rows] + products[0][2 * rows : 3 * rows]
        ) + (products[1][rows : 2 * rows] + products[1][3 * rows :])
        residual_now = target - (
            applied / token_total + ridge_term * iterate_half.astype(jnp.float32)
        )
        ratio_next = 1.0 / (2.0 * center / half_span - ratio_now)
        update = ratio_next * ratio_now * update + 2.0 * ratio_next / half_span * residual_now
        transform = transform + update
        ratio_now = ratio_next
    return transform


def solution(mesh):
    fine = Mesh(mesh.devices.reshape(SIZES), ALL)
    spec = P(FEAT, TOK)
    return jax.shard_map(
        body, mesh=fine, in_specs=(spec, spec), out_specs=spec, check_vma=False
    )
```

```python
import jax
import jax.numpy as jnp
import numpy as np
from jax import lax
from jax.sharding import Mesh, PartitionSpec as P

ITERS = 2
ridge_share = 0.2
TOK = ("yh", "x", "c")
FEAT = ("yl", "z")
ALL = TOK + FEAT
SIZES = (4, 4, 2, 2, 8)


def shift(array, axis, size, step):
    return lax.ppermute(array, axis, [(i, (i + step) % size) for i in range(size)])


def spread(array, axes, count):
    return lax.all_to_all(
        jnp.broadcast_to(array[None], (count,) + array.shape), axes, 0, 0
    )


def tile_moves():
    moves = []
    for yh in range(4):
        for x in range(4):
            for c in range(2):
                for yl in range(2):
                    for z in range(8):
                        other_yl, half = yh // 2, yh % 2
                        source = (((yh * 4 + x) * 2 + c) * 2 + yl) * 8 + z
                        to_z = (z + 4 * c + x) % 8
                        to_yh, to_x = other_yl * 2 + z // 4, z % 4
                        target = (((to_yh * 4 + to_x) * 2 + half) * 2 + yl) * 8 + to_z
                        moves.append((source, target))
    return moves


def body(entering, leaving):
    yl = lax.axis_index("yl")
    z = lax.axis_index("z")
    rows = entering.shape[0]
    quarter = rows // 4
    half_cols = rows // 2
    token_total = entering.shape[1] * 32
    order_all = rows * 16
    low = yl == 0

    pair = jnp.concatenate([entering, leaving], 0)
    other = shift(pair, "yl", 2, 1)
    first = jnp.where(low, pair, other)
    second = jnp.where(low, other, pair)
    columns = jnp.concatenate([first[:rows], second[:rows], first[rows:], second[rows:]], 0)

    blocks = {0: entering}
    up = down = entering
    for step in range(1, 5):
        down = shift(down, "z", 8, -1)
        blocks[step] = down
        if step < 4:
            up = shift(up, "z", 8, 1)
            blocks[8 - step] = up

    pieces = [
        lax.dot_general(
            blocks[s], columns, (((1,), (1,)), ((), ())), preferred_element_type=jnp.float32
        )
        for s in range(8)
    ]
    partial = jnp.stack(pieces).reshape(2, 4, rows, 4 * rows)
    partial = jnp.sum(lax.all_to_all(partial, "c", 0, 0), 0)
    partial = jnp.sum(lax.all_to_all(partial, "x", 0, 0), 0)
    packed = []
    for to_yh in range(4):
        for to_yl in range(2):
            top = half_cols * to_yl
            left = 2 * rows + half_cols * to_yh
            packed.append(
                jnp.concatenate(
                    [
                        partial[
                            quarter * to_yh : quarter * (to_yh + 1),
                            rows * to_yl : rows * (to_yl + 1),
                        ],
                        partial[top : top + quarter, left : left + half_cols],
                        partial[top + quarter : top + 2 * quarter, left : left + half_cols],
                    ],
                    1,
                )
            )
    own = lax.all_to_all(jnp.stack(packed), ("yh", "yl"), 0, 0)
    own = jnp.sum(own.reshape(4, 2, quarter, 2 * rows), 0)

    cross_own = jnp.concatenate([own[0, :, rows:], own[1, :, rows:]], 1)
    cross_own = lax.ppermute(cross_own, ALL, tile_moves()) / token_total
    cross_all = spread(cross_own, FEAT, 16).reshape(2, 8 * quarter, 2 * rows)
    target_all = jnp.concatenate(
        [
            cross_all[0, :, :rows],
            cross_all[1, :, :rows],
            cross_all[0, :, rows:],
            cross_all[1, :, rows:],
        ],
        1,
    )

    gram_part = jnp.concatenate([own[0, :, :rows], own[1, :, :rows]], 1)
    gram_part = spread(gram_part, "yh", 4)
    gram_part = jnp.concatenate([gram_part[q] for q in range(4)], 1)
    gram_part = spread(gram_part, "x", 4)
    gram = spread(gram_part, "c", 2).reshape(8 * quarter, 8 * rows)

    sums = jnp.sum(jnp.abs(gram), 0)
    row_peak = jnp.max(jnp.sum(sums.reshape(8, rows), 0))
    at_row = lax.broadcasted_iota(jnp.int32, (quarter, 8 * rows), 0)
    at_col = lax.broadcasted_iota(jnp.int32, (quarter, 8 * rows), 1)
    on_diagonal = at_col % (2 * rows) == rows * yl + quarter * (at_col // (2 * rows)) + at_row
    trace = jnp.sum(jnp.where(on_diagonal, gram[:quarter], 0.0))

    def halves(array):
        high = lax.reduce_precision(array, 8, 7)
        return high.astype(jnp.bfloat16), (array - high).astype(jnp.bfloat16)

    gram_high, gram_low = halves(gram)

    def turn(array):
        twice = jnp.concatenate([array, array], 0)
        return lax.dynamic_slice_in_dim(twice, quarter * z, 8 * quarter, 0)

    def times_gram(sides):
        product = 0.0
        for part in (gram_high, gram_low):
            for side in sides:
                wide = lax.dot_general(
                    part, side, (((0,), (0,)), ((), ())), preferred_element_type=jnp.float32
                )
                for q in range(4):
                    for k in range(2):
                        r0, c0 = (q * 2 + k) * rows, (k * 4 + q) * half_cols
                        product += wide[r0 : r0 + rows, c0 : c0 + half_cols]
        return jnp.concatenate([product[quarter * g : quarter * (g + 1)] for g in range(4)], 1)

    def own_tile(array):
        return lax.dynamic_slice(
            array, (quarter * z, 2 * rows * yl), (quarter, 2 * rows)
        )

    first_own = times_gram([turn(p) for p in halves(target_all)]) / token_total
    lane = lax.broadcasted_iota(jnp.int32, (quarter, 64), 1)
    tail = jnp.where(lane == 0, row_peak, trace)
    gathered = spread(jnp.concatenate([first_own, tail], 1), FEAT, 16)
    peak_all = jnp.max(gathered[:, 0, 2 * rows])
    energy = jnp.sum(gathered[:, 0, 2 * rows + 1])
    gathered = gathered.reshape(2, 8 * quarter, 2 * rows + 64)
    first_all = jnp.concatenate([gathered[0, :, : 2 * rows], gathered[1, :, : 2 * rows]], 1)

    ridge_term = ridge_share * energy / (token_total * order_all)
    upper_bound = peak_all / token_total + ridge_term
    center = (upper_bound + ridge_term) / 2.0
    half_span = (upper_bound - ridge_term) / 2.0

    ratio_now = half_span / center
    ratio_next = 1.0 / (2.0 * center / half_span - ratio_now)
    start = target_all / center
    residual = target_all - (first_all / center + ridge_term * start)
    update = ratio_next * ratio_now * start + 2.0 * ratio_next / half_span * residual
    transform = start + update
    ratio_now = ratio_next

    iterate_half = lax.reduce_precision(transform, 8, 7)
    applied = times_gram([turn(iterate_half.astype(jnp.bfloat16))]) / token_total
    residual = own_tile(target_all) - (applied + ridge_term * own_tile(iterate_half))
    ratio_next = 1.0 / (2.0 * center / half_span - ratio_now)
    final = own_tile(transform) + (
        ratio_next * ratio_now * own_tile(update) + 2.0 * ratio_next / half_span * residual
    )
    return jnp.concatenate(
        [final[:, half_cols * g : half_cols * (g + 1)] for g in range(4)], 0
    )


def solution(mesh):
    fine = Mesh(mesh.devices.reshape(SIZES), ALL)
    spec = P(FEAT, TOK)
    return jax.shard_map(
        body, mesh=fine, in_specs=(spec, spec), out_specs=spec, check_vma=False
    )
```

```python
import jax
import jax.numpy as jnp
import numpy as np
from jax import lax
from jax.sharding import Mesh, PartitionSpec as P

ITERS = 2
ridge_share = 0.2
TOK = ("yh", "x", "c")
FEAT = ("yl", "z")
ALL = TOK + FEAT
SIZES = (4, 4, 2, 2, 8)


def shift(array, axis, size, step):
    return lax.ppermute(array, axis, [(i, (i + step) % size) for i in range(size)])


def spread(array, axes, count):
    return lax.all_to_all(
        jnp.broadcast_to(array[None], (count,) + array.shape), axes, 0, 0
    )


def tile_moves():
    moves = []
    for yh in range(4):
        for x in range(4):
            for c in range(2):
                for yl in range(2):
                    for z in range(8):
                        other_yl, half = yh // 2, yh % 2
                        source = (((yh * 4 + x) * 2 + c) * 2 + yl) * 8 + z
                        to_z = (z + 4 * c + x) % 8
                        to_yh, to_x = other_yl * 2 + z // 4, z % 4
                        target = (((to_yh * 4 + to_x) * 2 + half) * 2 + yl) * 8 + to_z
                        moves.append((source, target))
    return moves


def body(entering, leaving):
    yl = lax.axis_index("yl")
    z = lax.axis_index("z")
    rows = entering.shape[0]
    quarter = rows // 4
    half_cols = rows // 2
    token_total = entering.shape[1] * 32
    order_all = rows * 16
    low = yl == 0

    pair = jnp.concatenate([entering, leaving], 0)
    other = shift(pair, "yl", 2, 1)
    first = jnp.where(low, pair, other)
    second = jnp.where(low, other, pair)
    columns = jnp.concatenate([first[:rows], second[:rows], first[rows:], second[rows:]], 0)

    blocks = {0: entering}
    up = down = entering
    for step in range(1, 5):
        down = shift(down, "z", 8, -1)
        blocks[step] = down
        if step < 4:
            up = shift(up, "z", 8, 1)
            blocks[8 - step] = up

    pieces = [
        lax.dot_general(
            blocks[s], columns, (((1,), (1,)), ((), ())), preferred_element_type=jnp.float32
        )
        for s in range(8)
    ]
    partial = jnp.stack(pieces).reshape(2, 4, rows, 4 * rows)
    partial = jnp.sum(lax.all_to_all(partial, "c", 0, 0), 0)
    partial = jnp.sum(lax.all_to_all(partial, "x", 0, 0), 0)
    packed = []
    for to_yh in range(4):
        for to_yl in range(2):
            top = half_cols * to_yl
            left = 2 * rows + half_cols * to_yh
            packed.append(
                jnp.concatenate(
                    [
                        partial[
                            quarter * to_yh : quarter * (to_yh + 1),
                            rows * to_yl : rows * (to_yl + 1),
                        ],
                        partial[top : top + quarter, left : left + half_cols],
                        partial[top + quarter : top + 2 * quarter, left : left + half_cols],
                    ],
                    1,
                )
            )
    own = lax.all_to_all(jnp.stack(packed), ("yh", "yl"), 0, 0)
    own = jnp.sum(own.reshape(4, 2, quarter, 2 * rows), 0)

    cross_own = jnp.concatenate([own[0, :, rows:], own[1, :, rows:]], 1)
    cross_own = lax.ppermute(cross_own, ALL, tile_moves()) / token_total
    gram_part = jnp.concatenate([own[0, :, :rows], own[1, :, :rows]], 1)
    cross_own, gram_part = lax.optimization_barrier((cross_own, gram_part))
    cross_all = lax.all_gather(jnp.concatenate([cross_own, gram_part[:, :192]], 1), FEAT, axis=0)[:, :, : 2 * rows].reshape(2, 8 * quarter, 2 * rows)
    target_all = jnp.concatenate(
        [
            cross_all[0, :, :rows],
            cross_all[1, :, :rows],
            cross_all[0, :, rows:],
            cross_all[1, :, rows:],
        ],
        1,
    )

    gram_part = spread(gram_part, "yh", 4)
    gram_part = jnp.concatenate([gram_part[q] for q in range(4)], 1)
    gram_part = spread(gram_part, "x", 4)
    gram = spread(gram_part, "c", 2).reshape(8 * quarter, 8 * rows)

    sums = jnp.sum(jnp.abs(gram), 0)
    row_peak = jnp.max(jnp.sum(sums.reshape(8, rows), 0))
    at_row = lax.broadcasted_iota(jnp.int32, (quarter, 8 * rows), 0)
    at_col = lax.broadcasted_iota(jnp.int32, (quarter, 8 * rows), 1)
    on_diagonal = at_col % (2 * rows) == rows * yl + quarter * (at_col // (2 * rows)) + at_row
    trace = jnp.sum(jnp.where(on_diagonal, gram[:quarter], 0.0))

    def halves(array):
        high = lax.reduce_precision(array, 8, 7)
        return high.astype(jnp.bfloat16), (array - high).astype(jnp.bfloat16)

    gram_high, gram_low = halves(gram)

    def turn(array):
        twice = jnp.concatenate([array, array], 0)
        return lax.dynamic_slice_in_dim(twice, quarter * z, 8 * quarter, 0)

    def times_gram(sides):
        product = 0.0
        for part in (gram_high, gram_low):
            for side in sides:
                wide = lax.dot_general(
                    part, side, (((0,), (0,)), ((), ())), preferred_element_type=jnp.float32
                )
                for q in range(4):
                    for k in range(2):
                        r0, c0 = (q * 2 + k) * rows, (k * 4 + q) * half_cols
                        product += wide[r0 : r0 + rows, c0 : c0 + half_cols]
        return jnp.concatenate([product[quarter * g : quarter * (g + 1)] for g in range(4)], 1)

    def own_tile(array):
        return lax.dynamic_slice(
            array, (quarter * z, 2 * rows * yl), (quarter, 2 * rows)
        )

    first_own = times_gram([turn(p) for p in halves(target_all)]) / token_total
    lane = lax.broadcasted_iota(jnp.int32, (quarter, 64), 1)
    tail = jnp.where(lane == 0, row_peak, trace)
    gathered = spread(jnp.concatenate([first_own, tail], 1), FEAT, 16)
    peak_all = jnp.max(gathered[:, 0, 2 * rows])
    energy = jnp.sum(gathered[:, 0, 2 * rows + 1])
    gathered = gathered.reshape(2, 8 * quarter, 2 * rows + 64)
    first_all = jnp.concatenate([gathered[0, :, : 2 * rows], gathered[1, :, : 2 * rows]], 1)

    ridge_term = ridge_share * energy / (token_total * order_all)
    upper_bound = peak_all / token_total + ridge_term
    center = (upper_bound + ridge_term) / 2.0
    half_span = (upper_bound - ridge_term) / 2.0

    ratio_now = half_span / center
    ratio_next = 1.0 / (2.0 * center / half_span - ratio_now)
    start = target_all / center
    residual = target_all - (first_all / center + ridge_term * start)
    update = ratio_next * ratio_now * start + 2.0 * ratio_next / half_span * residual
    transform = start + update
    ratio_now = ratio_next

    iterate_half = lax.reduce_precision(transform, 8, 7)
    applied = times_gram([turn(iterate_half.astype(jnp.bfloat16))]) / token_total
    residual = own_tile(target_all) - (applied + ridge_term * own_tile(iterate_half))
    ratio_next = 1.0 / (2.0 * center / half_span - ratio_now)
    final = own_tile(transform) + (
        ratio_next * ratio_now * own_tile(update) + 2.0 * ratio_next / half_span * residual
    )
    return jnp.concatenate(
        [final[:, half_cols * g : half_cols * (g + 1)] for g in range(4)], 0
    )


def solution(mesh):
    fine = Mesh(mesh.devices.reshape(SIZES), ALL)
    spec = P(FEAT, TOK)
    return jax.shard_map(
        body, mesh=fine, in_specs=(spec, spec), out_specs=spec, check_vma=False
    )
```

```python
import functools

import jax
import jax.numpy as jnp
from jax import lax
from jax.experimental import pallas as pl
from jax.experimental.pallas import tpu as pltpu
from jax.sharding import Mesh, PartitionSpec as P

ITERS = 2
ridge_share = 0.2
TOK = ("yh", "x", "c")
FEAT = ("yl", "z")
ALL = TOK + FEAT
SIZES = (4, 4, 2, 2, 8)


def shift(array, axis, size, step):
    return lax.ppermute(array, axis, [(i, (i + step) % size) for i in range(size)])


def spread(array, axes, count):
    return lax.all_to_all(
        jnp.broadcast_to(array[None], (count,) + array.shape), axes, 0, 0
    )


def tile_moves():
    moves = []
    for yh in range(4):
        for x in range(4):
            for c in range(2):
                for yl in range(2):
                    for z in range(8):
                        other_yl, half = yh // 2, yh % 2
                        source = (((yh * 4 + x) * 2 + c) * 2 + yl) * 8 + z
                        to_z = (z + 4 * c + x) % 8
                        to_yh, to_x = other_yl * 2 + z // 4, z % 4
                        target = (((to_yh * 4 + to_x) * 2 + half) * 2 + yl) * 8 + to_z
                        moves.append((source, target))
    return moves


def round_half(array):
    return array.astype(jnp.bfloat16).astype(jnp.float32)


def split_kernel(place, gram, target, high_out, low_out, sent):
    yl = place[0]
    rows, quarter = 160, 40
    sums = jnp.zeros((1, rows), jnp.float32)
    trace = jnp.zeros((1, 1), jnp.float32)
    at_row = lax.broadcasted_iota(jnp.int32, (quarter, rows), 0)
    at_col = lax.broadcasted_iota(jnp.int32, (quarter, rows), 1)
    for q in range(4):
        for k in range(2):
            n = q * 2 + k
            block = gram[:, :, n * rows : (n + 1) * rows].reshape(2 * rows, rows)
            sums += jnp.sum(jnp.abs(block), 0, keepdims=True)
            on_diagonal = (at_col == at_row + quarter * q) & (yl == k)
            trace += jnp.sum(jnp.where(on_diagonal, block[:quarter], 0.0), keepdims=True)
            high = block.astype(jnp.bfloat16)
            high_out[n * 2 * rows : (n + 1) * 2 * rows, :] = high
            low_out[n * 2 * rows : (n + 1) * 2 * rows, :] = (
                block - high.astype(jnp.float32)
            ).astype(jnp.bfloat16)
    peak = jnp.max(sums, keepdims=True)
    lane = lax.broadcasted_iota(jnp.int32, (quarter, 64), 1)
    value = jnp.where(lane < 3, peak, trace)
    first = round_half(value)
    second = round_half(value - first)
    third = value - first - second
    which = lane % 3
    tail = jnp.where(which == 0, first, jnp.where(which == 1, second, third))
    body_half = target[...].astype(jnp.bfloat16)
    tail_half = tail.astype(jnp.bfloat16)
    for d in range(16):
        sent[d, :, : 2 * rows] = body_half
        sent[d, :, 2 * rows :] = tail_half


def times_gram(z, got, high, low, seen):
    rows, quarter, half_cols = 160, 40, 80
    for k in range(2):
        for s in range(8):
            block = got[8 * k + lax.rem(z + s, 8)].astype(jnp.float32)
            for q in range(4):
                top = (q * 2 + k) * 2 * rows + s * quarter
                seen[top : top + quarter, :] = block[:, q * half_cols : (q + 1) * half_cols]
    side = seen[...].astype(jnp.bfloat16)
    product = 0.0
    for part in (high, low):
        product += lax.dot_general(
            part[...], side, (((0,), (0,)), ((), ())), preferred_element_type=jnp.float32
        )
    return jnp.concatenate([product[quarter * g : quarter * (g + 1)] for g in range(4)], 1)


def first_kernel(
    token_total, order_all, place, got, high, low, target_in, transform_out, update_out,
    sent, scalars, seen,
):
    rows = 160
    applied = times_gram(place[1], got, high, low, seen) / token_total
    peak_all = energy = None
    for d in range(16):
        tail = got[d][:, 2 * rows :].astype(jnp.float32)[:1]
        peak = tail[:, 0:1] + tail[:, 1:2] + tail[:, 2:3]
        trace = tail[:, 3:4] + tail[:, 4:5] + tail[:, 5:6]
        peak_all = peak if d == 0 else jnp.maximum(peak_all, peak)
        energy = trace if d == 0 else energy + trace
    ridge_term = ridge_share * energy / (token_total * order_all)
    upper_bound = peak_all / token_total + ridge_term
    center = (upper_bound + ridge_term) / 2.0
    half_span = (upper_bound - ridge_term) / 2.0
    ratio_now = half_span / center
    ratio_next = 1.0 / (2.0 * center / half_span - ratio_now)
    target = target_in[...]
    start = target / center
    residual = target - (applied + ridge_term * round_half(target)) / center
    update = ratio_next * ratio_now * start + 2.0 * ratio_next / half_span * residual
    transform = start + update
    ratio_last = 1.0 / (2.0 * center / half_span - ratio_next)
    transform_out[...] = transform
    update_out[...] = update
    lane = lax.broadcasted_iota(jnp.int32, (8, 128), 1)
    scalars[...] = jnp.where(
        lane == 0,
        ridge_term,
        jnp.where(lane == 1, ratio_last * ratio_next, 2.0 * ratio_last / half_span),
    )
    half = transform.astype(jnp.bfloat16)
    for d in range(16):
        sent[d, :, : 2 * rows] = half
        sent[d, :, 2 * rows :] = jnp.zeros((40, 64), jnp.bfloat16)


def second_kernel(
    token_total, place, got, high, low, target_in, transform_in, update_in, scalars, out, seen
):
    quarter, half_cols = 40, 80
    applied = times_gram(place[1], got, high, low, seen) / token_total
    ridge_term, keep, gain = scalars[0:1, 0:1], scalars[0:1, 1:2], scalars[0:1, 2:3]
    transform = transform_in[...]
    residual = target_in[...] - (applied + ridge_term * round_half(transform))
    final = transform + (keep * update_in[...] + gain * residual)
    for g in range(4):
        out[quarter * g : quarter * (g + 1), :] = final[:, half_cols * g : half_cols * (g + 1)]


def body(entering, leaving):
    yl = lax.axis_index("yl")
    z = lax.axis_index("z")
    rows = entering.shape[0]
    quarter = rows // 4
    half_cols = rows // 2
    token_total = entering.shape[1] * 32
    order_all = rows * 16
    low = yl == 0

    pair = jnp.concatenate([entering, leaving], 0)
    other = shift(pair, "yl", 2, 1)
    first = jnp.where(low, pair, other)
    second = jnp.where(low, other, pair)
    columns = jnp.concatenate([first[:rows], second[:rows], first[rows:], second[rows:]], 0)

    blocks = {0: entering}
    up = down = entering
    for step in range(1, 5):
        down = shift(down, "z", 8, -1)
        blocks[step] = down
        if step < 4:
            up = shift(up, "z", 8, 1)
            blocks[8 - step] = up

    pieces = [
        lax.dot_general(
            blocks[s], columns, (((1,), (1,)), ((), ())), preferred_element_type=jnp.float32
        )
        for s in range(8)
    ]
    partial = jnp.stack(pieces).reshape(2, 4, rows, 4 * rows)
    partial = jnp.sum(lax.all_to_all(partial, "c", 0, 0), 0)
    partial = jnp.sum(lax.all_to_all(partial, "x", 0, 0), 0)
    packed = []
    for to_yh in range(4):
        for to_yl in range(2):
            top = half_cols * to_yl
            left = 2 * rows + half_cols * to_yh
            packed.append(
                jnp.concatenate(
                    [
                        partial[
                            quarter * to_yh : quarter * (to_yh + 1),
                            rows * to_yl : rows * (to_yl + 1),
                        ],
                        partial[top : top + quarter, left : left + half_cols],
                        partial[top + quarter : top + 2 * quarter, left : left + half_cols],
                    ],
                    1,
                )
            )
    own = lax.all_to_all(jnp.stack(packed), ("yh", "yl"), 0, 0)
    own = jnp.sum(own.reshape(4, 2, quarter, 2 * rows), 0)

    cross_own = jnp.concatenate([own[0, :, rows:], own[1, :, rows:]], 1)
    cross_own = lax.ppermute(cross_own, ALL, tile_moves())
    cross_swap = shift(cross_own, "yl", 2, 1)
    target = jnp.where(
        low,
        jnp.concatenate([cross_own[:, :rows], cross_swap[:, :rows]], 1),
        jnp.concatenate([cross_swap[:, rows:], cross_own[:, rows:]], 1),
    ) / token_total

    gram_part = jnp.concatenate([own[0, :, :rows], own[1, :, :rows]], 1)
    gram_part = spread(gram_part, "yh", 4)
    gram_part = jnp.concatenate([gram_part[q] for q in range(4)], 1)
    gram_part = spread(gram_part, "x", 4)
    gram = spread(gram_part, "c", 2).reshape(8, quarter, 8 * rows)

    place = jnp.stack([yl, z]).astype(jnp.int32)
    vmem = pl.BlockSpec(memory_space=pltpu.VMEM)
    smem = pl.BlockSpec(memory_space=pltpu.SMEM)
    params = pltpu.CompilerParams(vmem_limit_bytes=40 * 2**20)
    tile = jax.ShapeDtypeStruct((quarter, 2 * rows), jnp.float32)
    message = jax.ShapeDtypeStruct((16, quarter, 2 * rows + 64), jnp.bfloat16)
    half_gram = jax.ShapeDtypeStruct((16 * rows, rows), jnp.bfloat16)
    columns_seen = pltpu.VMEM((16 * rows, half_cols), jnp.float32)
    gram_high, gram_low, sent = pl.pallas_call(
        split_kernel,
        out_shape=(half_gram, half_gram, message),
        in_specs=[smem, vmem, vmem],
        out_specs=(vmem, vmem, vmem),
        compiler_params=params,
    )(place, gram, target)
    got = lax.all_to_all(sent, FEAT, 0, 0)
    transform, update, sent, scalars = pl.pallas_call(
        functools.partial(first_kernel, token_total, order_all),
        out_shape=(tile, tile, message, jax.ShapeDtypeStruct((8, 128), jnp.float32)),
        in_specs=[smem] + [vmem] * 4,
        out_specs=(vmem,) * 4,
        scratch_shapes=[columns_seen],
        compiler_params=params,
    )(place, got, gram_high, gram_low, target)
    got = lax.all_to_all(sent, FEAT, 0, 0)
    return pl.pallas_call(
        functools.partial(second_kernel, token_total),
        out_shape=jax.ShapeDtypeStruct((rows, half_cols), jnp.float32),
        in_specs=[smem] + [vmem] * 7,
        out_specs=vmem,
        scratch_shapes=[columns_seen],
        compiler_params=params,
    )(place, got, gram_high, gram_low, target, transform, update, scalars)


def solution(mesh):
    fine = Mesh(mesh.devices.reshape(SIZES), ALL)
    spec = P(FEAT, TOK)
    return jax.shard_map(
        body, mesh=fine, in_specs=(spec, spec), out_specs=spec, check_vma=False
    )
```

```python
import functools

import jax
import jax.numpy as jnp
from jax import lax
from jax.experimental import pallas as pl
from jax.experimental.pallas import tpu as pltpu
from jax.sharding import Mesh, PartitionSpec as P

ITERS = 2
ridge_share = 0.2
TOK = ("yh", "x", "c")
FEAT = ("yl", "z")
ALL = TOK + FEAT
SIZES = (4, 4, 2, 2, 8)


def shift(array, axis, size, step):
    return lax.ppermute(array, axis, [(i, (i + step) % size) for i in range(size)])


def spread(array, axes, count):
    return lax.all_to_all(
        jnp.broadcast_to(array[None], (count,) + array.shape), axes, 0, 0
    )


def tile_moves():
    moves = []
    for yh in range(4):
        for x in range(4):
            for c in range(2):
                for yl in range(2):
                    for z in range(8):
                        other_yl, half = yh // 2, yh % 2
                        source = (((yh * 4 + x) * 2 + c) * 2 + yl) * 8 + z
                        to_z = 4 * c + x
                        to_yh, to_x = other_yl * 2 + z // 4, z % 4
                        target = (((to_yh * 4 + to_x) * 2 + half) * 2 + yl) * 8 + to_z
                        moves.append((source, target))
    return moves


def round_half(array):
    return array.astype(jnp.bfloat16).astype(jnp.float32)


def outer_kernel(place, block, pair, other, gram_out, cross_out, columns):
    rows, quarter, half_cols = 160, 40, 80

    @pl.when(pl.program_id(0) == 0)
    def _():
        low = place[0] == 0
        for part in range(2):
            here = slice(part * rows, (part + 1) * rows)
            mine, theirs = pair[here, :], other[here, :]
            top = part * 2 * rows
            columns[top : top + rows, :] = jnp.where(low, mine, theirs)
            columns[top + rows : top + 2 * rows, :] = jnp.where(low, theirs, mine)

    product = lax.dot_general(
        block[...], columns[...], (((1,), (1,)), ((), ())), preferred_element_type=jnp.float32
    )
    for n in range(2):
        one = product[n * rows : (n + 1) * rows]
        gram_out[n, :, : 2 * rows] = one[:half_cols, : 2 * rows]
        gram_out[n, :, 2 * rows :] = one[half_cols:, : 2 * rows]
        for q in range(4):
            left = 2 * rows + q * half_cols
            for g in range(4):
                cross_out[q, n, 0, :, g * half_cols : (g + 1) * half_cols] = one[
                    g * quarter : (g + 1) * quarter, left : left + half_cols
                ]


def split_kernel(place, gram, target, high_out, low_out, sent):
    yl, z = place[0], place[1]
    rows, quarter = 160, 40
    here = gram[z]
    sums = jnp.zeros((1, rows), jnp.float32)
    trace = jnp.zeros((1, 1), jnp.float32)
    at_row = lax.broadcasted_iota(jnp.int32, (quarter, rows), 0)
    at_col = lax.broadcasted_iota(jnp.int32, (quarter, rows), 1)
    for q in range(4):
        for k in range(2):
            n = q * 2 + k
            block = gram[:, :, n * rows : (n + 1) * rows].reshape(2 * rows, rows)
            sums += jnp.sum(jnp.abs(block), 0, keepdims=True)
            on_diagonal = (at_col == at_row + quarter * q) & (yl == k)
            own = here[:, n * rows : (n + 1) * rows]
            trace += jnp.sum(jnp.where(on_diagonal, own, 0.0), keepdims=True)
            high = block.astype(jnp.bfloat16)
            high_out[n * 2 * rows : (n + 1) * 2 * rows, :] = high
            low_out[n * 2 * rows : (n + 1) * 2 * rows, :] = (
                block - high.astype(jnp.float32)
            ).astype(jnp.bfloat16)
    peak = jnp.max(sums, keepdims=True)
    lane = lax.broadcasted_iota(jnp.int32, (quarter, 64), 1)
    value = jnp.where(lane < 3, peak, trace)
    first = round_half(value)
    second = round_half(value - first)
    third = value - first - second
    which = lane % 3
    tail = jnp.where(which == 0, first, jnp.where(which == 1, second, third))
    body_half = target[...].astype(jnp.bfloat16)
    tail_half = tail.astype(jnp.bfloat16)
    for d in range(16):
        sent[d, :, : 2 * rows] = body_half
        sent[d, :, 2 * rows :] = tail_half


def times_gram(got, high, low, seen):
    rows, quarter, half_cols = 160, 40, 80
    for k in range(2):
        for s in range(8):
            block = got[8 * k + s].astype(jnp.float32)
            for q in range(4):
                top = (q * 2 + k) * 2 * rows + s * quarter
                seen[top : top + quarter, :] = block[:, q * half_cols : (q + 1) * half_cols]
    side = seen[...].astype(jnp.bfloat16)
    product = 0.0
    for part in (high, low):
        product += lax.dot_general(
            part[...], side, (((0,), (0,)), ((), ())), preferred_element_type=jnp.float32
        )
    return jnp.concatenate([product[quarter * g : quarter * (g + 1)] for g in range(4)], 1)


def first_kernel(
    token_total, order_all, got, high, low, target_in, transform_out, update_out,
    sent, scalars, seen,
):
    rows = 160
    applied = times_gram(got, high, low, seen) / token_total
    peak_all = energy = None
    for d in range(16):
        tail = got[d][:, 2 * rows :].astype(jnp.float32)[:1]
        peak = tail[:, 0:1] + tail[:, 1:2] + tail[:, 2:3]
        trace = tail[:, 3:4] + tail[:, 4:5] + tail[:, 5:6]
        peak_all = peak if d == 0 else jnp.maximum(peak_all, peak)
        energy = trace if d == 0 else energy + trace
    ridge_term = ridge_share * energy / (token_total * order_all)
    upper_bound = peak_all / token_total + ridge_term
    center = (upper_bound + ridge_term) / 2.0
    half_span = (upper_bound - ridge_term) / 2.0
    ratio_now = half_span / center
    ratio_next = 1.0 / (2.0 * center / half_span - ratio_now)
    target = target_in[...]
    start = target / center
    residual = target - (applied + ridge_term * round_half(target)) / center
    update = ratio_next * ratio_now * start + 2.0 * ratio_next / half_span * residual
    transform = start + update
    ratio_last = 1.0 / (2.0 * center / half_span - ratio_next)
    transform_out[...] = transform
    update_out[...] = update
    lane = lax.broadcasted_iota(jnp.int32, (8, 128), 1)
    scalars[...] = jnp.where(
        lane == 0,
        ridge_term,
        jnp.where(lane == 1, ratio_last * ratio_next, 2.0 * ratio_last / half_span),
    )
    half = transform.astype(jnp.bfloat16)
    for d in range(16):
        sent[d, :, : 2 * rows] = half
        sent[d, :, 2 * rows :] = jnp.zeros((40, 64), jnp.bfloat16)


def second_kernel(
    token_total, got, high, low, target_in, transform_in, update_in, scalars, out, seen
):
    quarter, half_cols = 40, 80
    applied = times_gram(got, high, low, seen) / token_total
    ridge_term, keep, gain = scalars[0:1, 0:1], scalars[0:1, 1:2], scalars[0:1, 2:3]
    transform = transform_in[...]
    residual = target_in[...] - (applied + ridge_term * round_half(transform))
    final = transform + (keep * update_in[...] + gain * residual)
    for g in range(4):
        out[quarter * g : quarter * (g + 1), :] = final[:, half_cols * g : half_cols * (g + 1)]


def body(entering, leaving):
    yl = lax.axis_index("yl")
    z = lax.axis_index("z")
    rows = entering.shape[0]
    quarter = rows // 4
    half_cols = rows // 2
    token_total = entering.shape[1] * 32
    order_all = rows * 16

    place = jnp.stack([yl, z]).astype(jnp.int32)
    vmem = pl.BlockSpec(memory_space=pltpu.VMEM)
    smem = pl.BlockSpec(memory_space=pltpu.SMEM)
    params = pltpu.CompilerParams(vmem_limit_bytes=40 * 2**20)

    all_rows = lax.all_gather(entering, "z", axis=0, tiled=True)
    pair = jnp.concatenate([entering, leaving], 0)
    other = shift(pair, "yl", 2, 1)
    length = entering.shape[1]
    gram, cross = pl.pallas_call(
        outer_kernel,
        grid=(4,),
        out_shape=(
            jax.ShapeDtypeStruct((8, half_cols, 4 * rows), jnp.float32),
            jax.ShapeDtypeStruct((4, 4, 2, quarter, 2 * rows), jnp.float32),
        ),
        in_specs=[
            smem,
            pl.BlockSpec((2 * rows, length), lambda n: (n, 0)),
            pl.BlockSpec((2 * rows, length), lambda n: (0, 0)),
            pl.BlockSpec((2 * rows, length), lambda n: (0, 0)),
        ],
        out_specs=(
            pl.BlockSpec((2, half_cols, 4 * rows), lambda n: (n, 0, 0)),
            pl.BlockSpec((4, 2, 1, quarter, 2 * rows), lambda n: (0, n % 2, n // 2, 0, 0)),
        ),
        scratch_shapes=[pltpu.VMEM((4 * rows, length), jnp.bfloat16)],
        compiler_params=params,
    )(place, all_rows, pair, other)

    target = lax.psum_scatter(
        cross.reshape(32 * quarter, 2 * rows), TOK, scatter_dimension=0, tiled=True
    )

    gram = jnp.sum(lax.all_to_all(gram.reshape(2, 4, half_cols, 4 * rows), "c", 0, 0), 0)
    gram = jnp.sum(lax.all_to_all(gram, "x", 0, 0), 0)
    packed = []
    for to_yh in range(4):
        top, left = quarter * (to_yh % 2), 2 * rows * (to_yh // 2)
        for to_yl in range(2):
            at = left + rows * to_yl
            packed.append(gram[top : top + quarter, at : at + rows])
    own = lax.all_to_all(jnp.stack(packed), ("yh", "yl"), 0, 0)
    own = jnp.sum(own.reshape(4, 2, quarter, rows), 0)

    gram_part = jnp.concatenate([own[0], own[1]], 1)
    gram_part = spread(gram_part, "yh", 4)
    gram_part = jnp.concatenate([gram_part[q] for q in range(4)], 1)
    gram_part = lax.all_gather(gram_part, "x", axis=0)
    target, gram_part = lax.optimization_barrier((target, gram_part))
    target = lax.ppermute(target, ALL, tile_moves()) / token_total
    gram = spread(gram_part, "c", 2).reshape(8, quarter, 8 * rows)

    tile = jax.ShapeDtypeStruct((quarter, 2 * rows), jnp.float32)
    message = jax.ShapeDtypeStruct((16, quarter, 2 * rows + 64), jnp.bfloat16)
    half_gram = jax.ShapeDtypeStruct((16 * rows, rows), jnp.bfloat16)
    columns_seen = pltpu.VMEM((16 * rows, half_cols), jnp.float32)
    gram_high, gram_low, sent = pl.pallas_call(
        split_kernel,
        out_shape=(half_gram, half_gram, message),
        in_specs=[smem, vmem, vmem],
        out_specs=(vmem, vmem, vmem),
        compiler_params=params,
    )(place, gram, target)
    got = lax.all_to_all(sent, FEAT, 0, 0)
    transform, update, sent, scalars = pl.pallas_call(
        functools.partial(first_kernel, token_total, order_all),
        out_shape=(tile, tile, message, jax.ShapeDtypeStruct((8, 128), jnp.float32)),
        in_specs=[vmem] * 4,
        out_specs=(vmem,) * 4,
        scratch_shapes=[columns_seen],
        compiler_params=params,
    )(got, gram_high, gram_low, target)
    got = lax.all_to_all(sent, FEAT, 0, 0)
    return pl.pallas_call(
        functools.partial(second_kernel, token_total),
        out_shape=jax.ShapeDtypeStruct((rows, half_cols), jnp.float32),
        in_specs=[vmem] * 7,
        out_specs=vmem,
        scratch_shapes=[columns_seen],
        compiler_params=params,
    )(got, gram_high, gram_low, target, transform, update, scalars)


def solution(mesh):
    fine = Mesh(mesh.devices.reshape(SIZES), ALL)
    spec = P(FEAT, TOK)
    return jax.shard_map(
        body, mesh=fine, in_specs=(spec, spec), out_specs=spec, check_vma=False
    )
```

```python
import functools

import jax
import jax.numpy as jnp
from jax import lax
from jax.experimental import pallas as pl
from jax.experimental.pallas import tpu as pltpu
from jax.sharding import Mesh, PartitionSpec as P

ITERS = 2
ridge_share = 0.2
TOK = ("yh", "x", "c")
FEAT = ("yl", "z")
ALL = TOK + FEAT
SIZES = (4, 4, 2, 2, 8)


def shift(array, axis, size, step):
    return lax.ppermute(array, axis, [(i, (i + step) % size) for i in range(size)])


def spread(array, axes, count):
    return lax.all_to_all(
        jnp.broadcast_to(array[None], (count,) + array.shape), axes, 0, 0
    )


def tile_moves():
    moves = []
    for yh in range(4):
        for x in range(4):
            for c in range(2):
                for yl in range(2):
                    for z in range(8):
                        other_yl, half = yh // 2, yh % 2
                        source = (((yh * 4 + x) * 2 + c) * 2 + yl) * 8 + z
                        to_z = (z + 4 * c + x) % 8
                        to_yh, to_x = other_yl * 2 + z // 4, z % 4
                        target = (((to_yh * 4 + to_x) * 2 + half) * 2 + yl) * 8 + to_z
                        moves.append((source, target))
    return moves


def round_half(array):
    return array.astype(jnp.bfloat16).astype(jnp.float32)


def split_kernel(place, gram, target, high_out, low_out, sent):
    yl = place[0]
    rows, quarter = 160, 40
    sums = jnp.zeros((1, rows), jnp.float32)
    trace = jnp.zeros((1, 1), jnp.float32)
    at_row = lax.broadcasted_iota(jnp.int32, (quarter, rows), 0)
    at_col = lax.broadcasted_iota(jnp.int32, (quarter, rows), 1)
    for q in range(4):
        for k in range(2):
            n = q * 2 + k
            block = gram[:, :, n * rows : (n + 1) * rows].reshape(2 * rows, rows)
            sums += jnp.sum(jnp.abs(block), 0, keepdims=True)
            on_diagonal = (at_col == at_row + quarter * q) & (yl == k)
            trace += jnp.sum(jnp.where(on_diagonal, block[:quarter], 0.0), keepdims=True)
            high = block.astype(jnp.bfloat16)
            high_out[n * 2 * rows : (n + 1) * 2 * rows, :] = high
            low_out[n * 2 * rows : (n + 1) * 2 * rows, :] = (
                block - high.astype(jnp.float32)
            ).astype(jnp.bfloat16)
    peak = jnp.max(sums, keepdims=True)
    lane = lax.broadcasted_iota(jnp.int32, (quarter, 64), 1)
    value = jnp.where(lane < 3, peak, trace)
    first = round_half(value)
    second = round_half(value - first)
    third = value - first - second
    which = lane % 3
    tail = jnp.where(which == 0, first, jnp.where(which == 1, second, third))
    body_half = target[...].astype(jnp.bfloat16)
    tail_half = tail.astype(jnp.bfloat16)
    for d in range(16):
        sent[d, :, : 2 * rows] = body_half
        sent[d, :, 2 * rows :] = tail_half


def times_gram(z, got, high, low, seen):
    rows, quarter, half_cols = 160, 40, 80
    for k in range(2):
        for s in range(8):
            block = got[8 * k + lax.rem(z + s, 8)].astype(jnp.float32)
            for q in range(4):
                top = (q * 2 + k) * 2 * rows + s * quarter
                seen[top : top + quarter, :] = block[:, q * half_cols : (q + 1) * half_cols]
    side = seen[...].astype(jnp.bfloat16)
    product = 0.0
    for part in (high, low):
        product += lax.dot_general(
            part[...], side, (((0,), (0,)), ((), ())), preferred_element_type=jnp.float32
        )
    return jnp.concatenate([product[quarter * g : quarter * (g + 1)] for g in range(4)], 1)


def first_kernel(
    token_total, order_all, place, got, high, low, target_in, transform_out, update_out,
    sent, scalars, seen,
):
    rows = 160
    applied = times_gram(place[1], got, high, low, seen) / token_total
    peak_all = energy = None
    for d in range(16):
        tail = got[d][:, 2 * rows :].astype(jnp.float32)[:1]
        peak = tail[:, 0:1] + tail[:, 1:2] + tail[:, 2:3]
        trace = tail[:, 3:4] + tail[:, 4:5] + tail[:, 5:6]
        peak_all = peak if d == 0 else jnp.maximum(peak_all, peak)
        energy = trace if d == 0 else energy + trace
    ridge_term = ridge_share * energy / (token_total * order_all)
    upper_bound = peak_all / token_total + ridge_term
    center = (upper_bound + ridge_term) / 2.0
    half_span = (upper_bound - ridge_term) / 2.0
    ratio_now = half_span / center
    ratio_next = 1.0 / (2.0 * center / half_span - ratio_now)
    target = target_in[...]
    start = target / center
    residual = target - (applied + ridge_term * round_half(target)) / center
    update = ratio_next * ratio_now * start + 2.0 * ratio_next / half_span * residual
    transform = start + update
    ratio_last = 1.0 / (2.0 * center / half_span - ratio_next)
    transform_out[...] = transform
    update_out[...] = update
    lane = lax.broadcasted_iota(jnp.int32, (8, 128), 1)
    scalars[...] = jnp.where(
        lane == 0,
        ridge_term,
        jnp.where(lane == 1, ratio_last * ratio_next, 2.0 * ratio_last / half_span),
    )
    half = transform.astype(jnp.bfloat16)
    for d in range(16):
        sent[d, :, : 2 * rows] = half
        sent[d, :, 2 * rows :] = jnp.zeros((40, 64), jnp.bfloat16)


def second_kernel(
    token_total, place, got, high, low, target_in, transform_in, update_in, scalars, out, seen
):
    quarter, half_cols = 40, 80
    applied = times_gram(place[1], got, high, low, seen) / token_total
    ridge_term, keep, gain = scalars[0:1, 0:1], scalars[0:1, 1:2], scalars[0:1, 2:3]
    transform = transform_in[...]
    residual = target_in[...] - (applied + ridge_term * round_half(transform))
    final = transform + (keep * update_in[...] + gain * residual)
    for g in range(4):
        out[quarter * g : quarter * (g + 1), :] = final[:, half_cols * g : half_cols * (g + 1)]


def body(entering, leaving):
    yl = lax.axis_index("yl")
    z = lax.axis_index("z")
    rows = entering.shape[0]
    quarter = rows // 4
    half_cols = rows // 2
    token_total = entering.shape[1] * 32
    order_all = rows * 16
    low = yl == 0

    blocks = {0: entering}
    down = shift(entering, "z", 8, -1)
    up = shift(entering, "z", 8, 1)
    other_entering = shift(entering, "yl", 2, 1)
    down, up, other_entering, leaving = lax.optimization_barrier(
        (down, up, other_entering, leaving)
    )
    blocks[1], blocks[7] = down, up
    down, up = shift(down, "z", 8, -1), shift(up, "z", 8, 1)
    other_leaving = shift(leaving, "yl", 2, 1)
    down, up, other_leaving = lax.optimization_barrier((down, up, other_leaving))
    blocks[2], blocks[6] = down, up
    down, up = lax.optimization_barrier((shift(down, "z", 8, -1), shift(up, "z", 8, 1)))
    blocks[3], blocks[5] = down, up
    blocks[4] = shift(down, "z", 8, -1)
    columns = jnp.concatenate(
        [
            jnp.where(low, entering, other_entering),
            jnp.where(low, other_entering, entering),
            jnp.where(low, leaving, other_leaving),
            jnp.where(low, other_leaving, leaving),
        ],
        0,
    )

    pieces = [
        lax.dot_general(
            blocks[s], columns, (((1,), (1,)), ((), ())), preferred_element_type=jnp.float32
        )
        for s in range(8)
    ]
    partial = jnp.stack(pieces).reshape(2, 4, rows, 4 * rows)
    partial = jnp.sum(lax.all_to_all(partial, "c", 0, 0), 0)
    partial = jnp.sum(lax.all_to_all(partial, "x", 0, 0), 0)
    packed = []
    for to_yh in range(4):
        for to_yl in range(2):
            top = half_cols * to_yl
            left = 2 * rows + half_cols * to_yh
            packed.append(
                jnp.concatenate(
                    [
                        partial[
                            quarter * to_yh : quarter * (to_yh + 1),
                            rows * to_yl : rows * (to_yl + 1),
                        ],
                        partial[top : top + quarter, left : left + half_cols],
                        partial[top + quarter : top + 2 * quarter, left : left + half_cols],
                    ],
                    1,
                )
            )
    own = lax.all_to_all(jnp.stack(packed), ("yh", "yl"), 0, 0)
    own = jnp.sum(own.reshape(4, 2, quarter, 2 * rows), 0)

    cross_own = jnp.concatenate([own[0, :, rows:], own[1, :, rows:]], 1)
    cross_own = lax.ppermute(cross_own, ALL, tile_moves())
    cross_swap = shift(cross_own, "yl", 2, 1)
    target = jnp.where(
        low,
        jnp.concatenate([cross_own[:, :rows], cross_swap[:, :rows]], 1),
        jnp.concatenate([cross_swap[:, rows:], cross_own[:, rows:]], 1),
    ) / token_total

    gram_part = jnp.concatenate([own[0, :, :rows], own[1, :, :rows]], 1)
    gram_part = spread(gram_part, "yh", 4)
    gram_part = jnp.concatenate([gram_part[q] for q in range(4)], 1)
    gram_part = spread(gram_part, "x", 4)
    gram = spread(gram_part, "c", 2).reshape(8, quarter, 8 * rows)

    place = jnp.stack([yl, z]).astype(jnp.int32)
    vmem = pl.BlockSpec(memory_space=pltpu.VMEM)
    smem = pl.BlockSpec(memory_space=pltpu.SMEM)
    params = pltpu.CompilerParams(vmem_limit_bytes=40 * 2**20)
    tile = jax.ShapeDtypeStruct((quarter, 2 * rows), jnp.float32)
    message = jax.ShapeDtypeStruct((16, quarter, 2 * rows + 64), jnp.bfloat16)
    half_gram = jax.ShapeDtypeStruct((16 * rows, rows), jnp.bfloat16)
    columns_seen = pltpu.VMEM((16 * rows, half_cols), jnp.float32)
    gram_high, gram_low, sent = pl.pallas_call(
        split_kernel,
        out_shape=(half_gram, half_gram, message),
        in_specs=[smem, vmem, vmem],
        out_specs=(vmem, vmem, vmem),
        compiler_params=params,
    )(place, gram, target)
    got = lax.all_to_all(sent, FEAT, 0, 0)
    transform, update, sent, scalars = pl.pallas_call(
        functools.partial(first_kernel, token_total, order_all),
        out_shape=(tile, tile, message, jax.ShapeDtypeStruct((8, 128), jnp.float32)),
        in_specs=[smem] + [vmem] * 4,
        out_specs=(vmem,) * 4,
        scratch_shapes=[columns_seen],
        compiler_params=params,
    )(place, got, gram_high, gram_low, target)
    got = lax.all_to_all(sent, FEAT, 0, 0)
    return pl.pallas_call(
        functools.partial(second_kernel, token_total),
        out_shape=jax.ShapeDtypeStruct((rows, half_cols), jnp.float32),
        in_specs=[smem] + [vmem] * 7,
        out_specs=vmem,
        scratch_shapes=[columns_seen],
        compiler_params=params,
    )(place, got, gram_high, gram_low, target, transform, update, scalars)


def solution(mesh):
    fine = Mesh(mesh.devices.reshape(SIZES), ALL)
    spec = P(FEAT, TOK)
    return jax.shard_map(
        body, mesh=fine, in_specs=(spec, spec), out_specs=spec, check_vma=False
    )
```

```python
import functools

import jax
import jax.numpy as jnp
from jax import lax
from jax.experimental import pallas as pl
from jax.experimental.pallas import tpu as pltpu
from jax.sharding import Mesh, PartitionSpec as P

ITERS = 2
ridge_share = 0.2
TOK = ("yh", "x", "c")
FEAT = ("yl", "z")
ALL = TOK + FEAT
SIZES = (4, 4, 2, 2, 8)


def shift(array, axis, size, step):
    return lax.ppermute(array, axis, [(i, (i + step) % size) for i in range(size)])


def spread(array, axes, count):
    return lax.all_to_all(
        jnp.broadcast_to(array[None], (count,) + array.shape), axes, 0, 0
    )


def tile_moves(flip):
    moves = []
    for yh in range(4):
        for x in range(4):
            for c in range(2):
                for yl in range(2):
                    for z in range(8):
                        other_yl, half = yh // 2, yh % 2
                        source = (((yh * 4 + x) * 2 + c) * 2 + yl) * 8 + z
                        to_yl = (x % 2) ^ flip
                        to_z = (z + 7 + 4 * yl + 2 * c + x // 2) % 8
                        to_yh, to_x = other_yl * 2 + z // 4, z % 4
                        target = (((to_yh * 4 + to_x) * 2 + half) * 2 + to_yl) * 8 + to_z
                        moves.append((source, target))
    return moves


def round_half(array):
    return array.astype(jnp.bfloat16).astype(jnp.float32)


def split_kernel(place, gram, target, high_out, low_out, sent):
    yl = place[0]
    rows, quarter = 160, 40
    sums = jnp.zeros((1, rows), jnp.float32)
    trace = jnp.zeros((1, 1), jnp.float32)
    at_row = lax.broadcasted_iota(jnp.int32, (quarter, rows), 0)
    at_col = lax.broadcasted_iota(jnp.int32, (quarter, rows), 1)
    for q in range(4):
        for k in range(2):
            n = q * 2 + k
            block = gram[:, :, n * rows : (n + 1) * rows].reshape(2 * rows, rows)
            sums += jnp.sum(jnp.abs(block), 0, keepdims=True)
            if q < 2:
                for m in range(2):
                    own = block[(2 + m) * quarter : (3 + m) * quarter]
                    on_diagonal = (at_col == at_row + 80 * m + quarter * q) & (yl == k)
                    trace += jnp.sum(jnp.where(on_diagonal, own, 0.0), keepdims=True)
            high = block.astype(jnp.bfloat16)
            high_out[n * 2 * rows : (n + 1) * 2 * rows, :] = high
            low_out[n * 2 * rows : (n + 1) * 2 * rows, :] = (
                block - high.astype(jnp.float32)
            ).astype(jnp.bfloat16)
    peak = jnp.max(sums, keepdims=True)
    lane = lax.broadcasted_iota(jnp.int32, (quarter, 64), 1)
    value = jnp.where(lane < 3, peak, trace)
    first = round_half(value)
    second = round_half(value - first)
    third = value - first - second
    which = lane % 3
    tail = jnp.where(which == 0, first, jnp.where(which == 1, second, third))
    body_half = target[...].astype(jnp.bfloat16)
    tail_half = tail.astype(jnp.bfloat16)
    for d in range(16):
        sent[d, :, : 2 * rows] = body_half
        sent[d, :, 2 * rows :] = tail_half


def times_gram(z, got, high, low, seen):
    rows, quarter, half_cols = 160, 40, 80
    for k in range(2):
        for s in range(8):
            p, c, l = s // 4, s // 2 % 2, s % 2
            block = got[8 * k + lax.rem(z + 7 + s, 8)].astype(jnp.float32)
            for m in range(2):
                for a in range(2):
                    g = 2 * m + a
                    top = ((2 * p + a) * 2 + k) * 2 * rows + (4 * c + 2 * l + m) * quarter
                    seen[top : top + quarter, :] = block[:, g * half_cols : (g + 1) * half_cols]
    side = seen[...].astype(jnp.bfloat16)
    product = 0.0
    for part in (high, low):
        product += lax.dot_general(
            part[...], side, (((0,), (0,)), ((), ())), preferred_element_type=jnp.float32
        )
    return jnp.concatenate([product[quarter * g : quarter * (g + 1)] for g in range(4)], 1)


def first_kernel(
    token_total, order_all, place, got, high, low, target_in, transform_out, update_out,
    sent, scalars, seen,
):
    rows = 160
    applied = times_gram(place[1], got, high, low, seen) / token_total
    peak_all = energy = None
    for d in range(16):
        tail = got[d][:, 2 * rows :].astype(jnp.float32)[:1]
        peak = tail[:, 0:1] + tail[:, 1:2] + tail[:, 2:3]
        trace = tail[:, 3:4] + tail[:, 4:5] + tail[:, 5:6]
        peak_all = peak if d == 0 else jnp.maximum(peak_all, peak)
        energy = trace if d == 0 else energy + trace
    ridge_term = ridge_share * energy / (token_total * order_all)
    upper_bound = peak_all / token_total + ridge_term
    center = (upper_bound + ridge_term) / 2.0
    half_span = (upper_bound - ridge_term) / 2.0
    ratio_now = half_span / center
    ratio_next = 1.0 / (2.0 * center / half_span - ratio_now)
    target = target_in[...]
    start = target / center
    residual = target - (applied + ridge_term * round_half(target)) / center
    update = ratio_next * ratio_now * start + 2.0 * ratio_next / half_span * residual
    transform = start + update
    ratio_last = 1.0 / (2.0 * center / half_span - ratio_next)
    transform_out[...] = transform
    update_out[...] = update
    lane = lax.broadcasted_iota(jnp.int32, (8, 128), 1)
    scalars[...] = jnp.where(
        lane == 0,
        ridge_term,
        jnp.where(lane == 1, ratio_last * ratio_next, 2.0 * ratio_last / half_span),
    )
    half = transform.astype(jnp.bfloat16)
    for d in range(16):
        sent[d, :, : 2 * rows] = half
        sent[d, :, 2 * rows :] = jnp.zeros((40, 64), jnp.bfloat16)


def second_kernel(
    token_total, place, got, high, low, target_in, transform_in, update_in, scalars, out, seen
):
    quarter, half_cols = 40, 80
    applied = times_gram(place[1], got, high, low, seen) / token_total
    ridge_term, keep, gain = scalars[0:1, 0:1], scalars[0:1, 1:2], scalars[0:1, 2:3]
    transform = transform_in[...]
    residual = target_in[...] - (applied + ridge_term * round_half(transform))
    final = transform + (keep * update_in[...] + gain * residual)
    for g in range(4):
        out[quarter * g : quarter * (g + 1), :] = final[:, half_cols * g : half_cols * (g + 1)]


def body(entering, leaving):
    yl = lax.axis_index("yl")
    z = lax.axis_index("z")
    rows = entering.shape[0]
    quarter = rows // 4
    half_cols = rows // 2
    token_total = entering.shape[1] * 32
    order_all = rows * 16
    low = yl == 0

    pair = jnp.concatenate([entering, leaving], 0)
    other = shift(pair, "yl", 2, 1)
    first = jnp.where(low, pair, other)
    second = jnp.where(low, other, pair)
    columns = jnp.concatenate([first[:rows], second[:rows], first[rows:], second[rows:]], 0)

    def products(blocks):
        return jnp.stack(
            [
                lax.dot_general(
                    block, columns, (((1,), (1,)), ((), ())), preferred_element_type=jnp.float32
                )
                for block in blocks
            ]
        )

    def core_sum(array):
        array = lax.all_to_all(array.reshape(2, 2, rows, 4 * rows), "c", 0, 0)
        return jnp.sum(array, 0).reshape(4, half_cols, 4 * rows)

    down_1, up_1 = shift(entering, "z", 8, -1), shift(entering, "z", 8, 1)
    down_2, up_2 = shift(down_1, "z", 8, -1), shift(up_1, "z", 8, 1)
    down_3 = shift(down_2, "z", 8, -1)
    early = core_sum(products([up_1, entering, down_1, down_2]))
    early, down_3, up_2 = lax.optimization_barrier((early, down_3, up_2))
    early = lax.all_to_all(early, "x", 0, 0)
    down_4, up_3 = shift(down_3, "z", 8, -1), shift(up_2, "z", 8, 1)
    early, down_4, up_3 = lax.optimization_barrier((early, down_4, up_3))
    late = core_sum(products([down_3, down_4, up_3, up_2]))
    late = lax.all_to_all(late, "x", 0, 0)
    sums = (jnp.sum(early, 0), jnp.sum(late, 0))
    packed = []
    for to_yh in range(4):
        gram_from, top = sums[to_yh // 2], quarter * (to_yh % 2)
        left = 2 * rows + half_cols * to_yh
        for to_yl in range(2):
            packed.append(
                jnp.concatenate(
                    [
                        gram_from[top : top + quarter, rows * to_yl : rows * (to_yl + 1)],
                        sums[to_yl][:quarter, left : left + half_cols],
                        sums[to_yl][quarter:, left : left + half_cols],
                    ],
                    1,
                )
            )
    own = lax.all_to_all(jnp.stack(packed), ("yh", "yl"), 0, 0)
    own = jnp.sum(own.reshape(4, 2, quarter, 2 * rows), 0)

    even = (lax.axis_index("x") & 1) == 0
    near = jnp.where(even, own[0, :, rows:], own[1, :, rows:])
    far = jnp.where(even, own[1, :, rows:], own[0, :, rows:])
    near = lax.ppermute(near, ALL, tile_moves(0))
    far = lax.ppermute(far, ALL, tile_moves(1))
    target = (
        jnp.concatenate([jnp.where(low, near, far), jnp.where(low, far, near)], 1) / token_total
    )

    gram_part = jnp.concatenate([own[0, :, :rows], own[1, :, :rows]], 1)
    gram_part = spread(gram_part, "yh", 4)
    gram_part = jnp.concatenate([gram_part[q] for q in range(4)], 1)
    gram_part = spread(gram_part, "x", 4)
    gram = spread(gram_part, "c", 2).reshape(8, quarter, 8 * rows)

    place = jnp.stack([yl, z]).astype(jnp.int32)
    vmem = pl.BlockSpec(memory_space=pltpu.VMEM)
    smem = pl.BlockSpec(memory_space=pltpu.SMEM)
    params = pltpu.CompilerParams(vmem_limit_bytes=40 * 2**20)
    tile = jax.ShapeDtypeStruct((quarter, 2 * rows), jnp.float32)
    message = jax.ShapeDtypeStruct((16, quarter, 2 * rows + 64), jnp.bfloat16)
    half_gram = jax.ShapeDtypeStruct((16 * rows, rows), jnp.bfloat16)
    columns_seen = pltpu.VMEM((16 * rows, half_cols), jnp.float32)
    gram_high, gram_low, sent = pl.pallas_call(
        split_kernel,
        out_shape=(half_gram, half_gram, message),
        in_specs=[smem, vmem, vmem],
        out_specs=(vmem, vmem, vmem),
        compiler_params=params,
    )(place, gram, target)
    got = lax.all_to_all(sent, FEAT, 0, 0)
    transform, update, sent, scalars = pl.pallas_call(
        functools.partial(first_kernel, token_total, order_all),
        out_shape=(tile, tile, message, jax.ShapeDtypeStruct((8, 128), jnp.float32)),
        in_specs=[smem] + [vmem] * 4,
        out_specs=(vmem,) * 4,
        scratch_shapes=[columns_seen],
        compiler_params=params,
    )(place, got, gram_high, gram_low, target)
    got = lax.all_to_all(sent, FEAT, 0, 0)
    return pl.pallas_call(
        functools.partial(second_kernel, token_total),
        out_shape=jax.ShapeDtypeStruct((rows, half_cols), jnp.float32),
        in_specs=[smem] + [vmem] * 7,
        out_specs=vmem,
        scratch_shapes=[columns_seen],
        compiler_params=params,
    )(place, got, gram_high, gram_low, target, transform, update, scalars)


def solution(mesh):
    fine = Mesh(mesh.devices.reshape(SIZES), ALL)
    spec = P(FEAT, TOK)
    return jax.shard_map(
        body, mesh=fine, in_specs=(spec, spec), out_specs=spec, check_vma=False
    )
```

```python
import functools

import jax
import jax.numpy as jnp
from jax import lax
from jax.experimental import pallas as pl
from jax.experimental.pallas import tpu as pltpu
from jax.sharding import Mesh, PartitionSpec as P

ITERS = 2
ridge_share = 0.2
TOK = ("yh", "x", "c")
FEAT = ("yl", "z")
ALL = TOK + FEAT
SIZES = (4, 4, 2, 2, 8)


def shift(array, axis, size, step):
    return lax.ppermute(array, axis, [(i, (i + step) % size) for i in range(size)])


def spread(array, axes, count):
    return lax.all_to_all(
        jnp.broadcast_to(array[None], (count,) + array.shape), axes, 0, 0
    )


def tile_moves(flip):
    moves = []
    for yh in range(4):
        for x in range(4):
            for c in range(2):
                for yl in range(2):
                    for z in range(8):
                        other_yl, half = yh // 2, yh % 2
                        source = (((yh * 4 + x) * 2 + c) * 2 + yl) * 8 + z
                        to_yl = (x % 2) ^ flip
                        to_z = (z + 7 + 4 * yl + 2 * c + x // 2) % 8
                        to_yh, to_x = other_yl * 2 + z // 4, z % 4
                        target = (((to_yh * 4 + to_x) * 2 + half) * 2 + to_yl) * 8 + to_z
                        moves.append((source, target))
    return moves


def round_half(array):
    return array.astype(jnp.bfloat16).astype(jnp.float32)


def pack_kernel(early, late, packed):
    rows, quarter, half_cols = 160, 40, 80
    sums = [(part[0] + part[1]) + (part[2] + part[3]) for part in (early, late)]
    for to_yh in range(4):
        gram_from, top = sums[to_yh // 2], quarter * (to_yh % 2)
        left = 2 * rows + half_cols * to_yh
        for to_yl in range(2):
            to = 2 * to_yh + to_yl
            packed[to, :, :rows] = gram_from[
                top : top + quarter, rows * to_yl : rows * (to_yl + 1)
            ]
            for n in range(2):
                at = rows + half_cols * n
                packed[to, :, at : at + half_cols] = sums[to_yl][
                    quarter * n : quarter * (n + 1), left : left + half_cols
                ]


def split_kernel(place, gram, target, high_out, low_out, sent):
    yl = place[0]
    rows, quarter = 160, 40
    sums = jnp.zeros((1, rows), jnp.float32)
    trace = jnp.zeros((1, 1), jnp.float32)
    at_row = lax.broadcasted_iota(jnp.int32, (quarter, rows), 0)
    at_col = lax.broadcasted_iota(jnp.int32, (quarter, rows), 1)
    for q in range(4):
        for k in range(2):
            n = q * 2 + k
            block = gram[:, :, n * rows : (n + 1) * rows].reshape(2 * rows, rows)
            sums += jnp.sum(jnp.abs(block), 0, keepdims=True)
            if q < 2:
                for m in range(2):
                    own = block[(2 + m) * quarter : (3 + m) * quarter]
                    on_diagonal = (at_col == at_row + 80 * m + quarter * q) & (yl == k)
                    trace += jnp.sum(jnp.where(on_diagonal, own, 0.0), keepdims=True)
            high = block.astype(jnp.bfloat16)
            high_out[n * 2 * rows : (n + 1) * 2 * rows, :] = high
            low_out[n * 2 * rows : (n + 1) * 2 * rows, :] = (
                block - high.astype(jnp.float32)
            ).astype(jnp.bfloat16)
    peak = jnp.max(sums, keepdims=True)
    lane = lax.broadcasted_iota(jnp.int32, (quarter, 64), 1)
    value = jnp.where(lane < 3, peak, trace)
    first = round_half(value)
    second = round_half(value - first)
    third = value - first - second
    which = lane % 3
    tail = jnp.where(which == 0, first, jnp.where(which == 1, second, third))
    body_half = target[...].astype(jnp.bfloat16)
    tail_half = tail.astype(jnp.bfloat16)
    for d in range(16):
        sent[d, :, : 2 * rows] = body_half
        sent[d, :, 2 * rows :] = tail_half


def times_gram(z, got, high, low, seen):
    rows, quarter, half_cols = 160, 40, 80
    for k in range(2):
        for s in range(8):
            p, c, l = s // 4, s // 2 % 2, s % 2
            block = got[8 * k + lax.rem(z + 7 + s, 8)].astype(jnp.float32)
            for m in range(2):
                for a in range(2):
                    g = 2 * m + a
                    top = ((2 * p + a) * 2 + k) * 2 * rows + (4 * c + 2 * l + m) * quarter
                    seen[top : top + quarter, :] = block[:, g * half_cols : (g + 1) * half_cols]
    side = seen[...].astype(jnp.bfloat16)
    product = 0.0
    for part in (high, low):
        product += lax.dot_general(
            part[...], side, (((0,), (0,)), ((), ())), preferred_element_type=jnp.float32
        )
    return jnp.concatenate([product[quarter * g : quarter * (g + 1)] for g in range(4)], 1)


def first_kernel(
    token_total, order_all, place, got, high, low, target_in, transform_out, update_out,
    sent, scalars, seen,
):
    rows = 160
    applied = times_gram(place[1], got, high, low, seen) / token_total
    peak_all = energy = None
    for d in range(16):
        tail = got[d][:, 2 * rows :].astype(jnp.float32)[:1]
        peak = tail[:, 0:1] + tail[:, 1:2] + tail[:, 2:3]
        trace = tail[:, 3:4] + tail[:, 4:5] + tail[:, 5:6]
        peak_all = peak if d == 0 else jnp.maximum(peak_all, peak)
        energy = trace if d == 0 else energy + trace
    ridge_term = ridge_share * energy / (token_total * order_all)
    upper_bound = peak_all / token_total + ridge_term
    center = (upper_bound + ridge_term) / 2.0
    half_span = (upper_bound - ridge_term) / 2.0
    ratio_now = half_span / center
    ratio_next = 1.0 / (2.0 * center / half_span - ratio_now)
    target = target_in[...]
    start = target / center
    residual = target - (applied + ridge_term * round_half(target)) / center
    update = ratio_next * ratio_now * start + 2.0 * ratio_next / half_span * residual
    transform = start + update
    ratio_last = 1.0 / (2.0 * center / half_span - ratio_next)
    transform_out[...] = transform
    update_out[...] = update
    lane = lax.broadcasted_iota(jnp.int32, (8, 128), 1)
    scalars[...] = jnp.where(
        lane == 0,
        ridge_term,
        jnp.where(lane == 1, ratio_last * ratio_next, 2.0 * ratio_last / half_span),
    )
    half = transform.astype(jnp.bfloat16)
    for d in range(16):
        sent[d, :, : 2 * rows] = half
        sent[d, :, 2 * rows :] = jnp.zeros((40, 64), jnp.bfloat16)


def second_kernel(
    token_total, place, got, high, low, target_in, transform_in, update_in, scalars, out, seen
):
    quarter, half_cols = 40, 80
    applied = times_gram(place[1], got, high, low, seen) / token_total
    ridge_term, keep, gain = scalars[0:1, 0:1], scalars[0:1, 1:2], scalars[0:1, 2:3]
    transform = transform_in[...]
    residual = target_in[...] - (applied + ridge_term * round_half(transform))
    final = transform + (keep * update_in[...] + gain * residual)
    for g in range(4):
        out[quarter * g : quarter * (g + 1), :] = final[:, half_cols * g : half_cols * (g + 1)]


def body(entering, leaving):
    yl = lax.axis_index("yl")
    z = lax.axis_index("z")
    rows = entering.shape[0]
    quarter = rows // 4
    half_cols = rows // 2
    token_total = entering.shape[1] * 32
    order_all = rows * 16
    low = yl == 0

    pair = jnp.concatenate([entering, leaving], 0)
    other = shift(pair, "yl", 2, 1)
    first = jnp.where(low, pair, other)
    second = jnp.where(low, other, pair)
    columns = jnp.concatenate([first[:rows], second[:rows], first[rows:], second[rows:]], 0)

    def products(blocks, order):
        whole = jnp.zeros((len(blocks), rows, 4 * rows), jnp.float32)
        for n in order:
            product = lax.dot_general(
                blocks[n], columns, (((1,), (1,)), ((), ())), preferred_element_type=jnp.float32
            )
            whole = lax.dynamic_update_index_in_dim(whole, product, n, 0)
        return whole

    def core_sum(array):
        array = lax.all_to_all(array.reshape(2, 2, rows, 4 * rows), "c", 0, 0)
        return jnp.sum(array, 0).reshape(4, half_cols, 4 * rows)

    down_1, up_1 = shift(entering, "z", 8, -1), shift(entering, "z", 8, 1)
    down_2, up_2 = shift(down_1, "z", 8, -1), shift(up_1, "z", 8, 1)
    down_3 = shift(down_2, "z", 8, -1)
    early = core_sum(products([up_1, entering, down_1, down_2], (1, 0, 2, 3)))
    early, down_3, up_2 = lax.optimization_barrier((early, down_3, up_2))
    early = lax.all_to_all(early, "x", 0, 0)
    down_4, up_3 = shift(down_3, "z", 8, -1), shift(up_2, "z", 8, 1)
    early, down_4, up_3 = lax.optimization_barrier((early, down_4, up_3))
    late = core_sum(products([down_3, down_4, up_3, up_2], (0, 3, 1, 2)))
    late = lax.all_to_all(late, "x", 0, 0)
    packed = pl.pallas_call(
        pack_kernel,
        out_shape=jax.ShapeDtypeStruct((8, quarter, 2 * rows), jnp.float32),
        in_specs=[pl.BlockSpec(memory_space=pltpu.VMEM)] * 2,
        out_specs=pl.BlockSpec(memory_space=pltpu.VMEM),
        compiler_params=pltpu.CompilerParams(vmem_limit_bytes=40 * 2**20),
    )(early, late)
    own = lax.all_to_all(packed, ("yh", "yl"), 0, 0)
    own = jnp.sum(own.reshape(4, 2, quarter, 2 * rows), 0)

    even = (lax.axis_index("x") & 1) == 0
    near = jnp.where(even, own[0, :, rows:], own[1, :, rows:])
    far = jnp.where(even, own[1, :, rows:], own[0, :, rows:])
    near = lax.ppermute(near, ALL, tile_moves(0))
    far = lax.ppermute(far, ALL, tile_moves(1))
    target = (
        jnp.concatenate([jnp.where(low, near, far), jnp.where(low, far, near)], 1) / token_total
    )

    gram_part = jnp.concatenate([own[0, :, :rows], own[1, :, :rows]], 1)
    gram_part = spread(gram_part, "yh", 4)
    gram_part = jnp.concatenate([gram_part[q] for q in range(4)], 1)
    gram_part = spread(gram_part, "x", 4)
    gram = spread(gram_part, "c", 2).reshape(8, quarter, 8 * rows)

    place = jnp.stack([yl, z]).astype(jnp.int32)
    vmem = pl.BlockSpec(memory_space=pltpu.VMEM)
    smem = pl.BlockSpec(memory_space=pltpu.SMEM)
    params = pltpu.CompilerParams(vmem_limit_bytes=40 * 2**20)
    tile = jax.ShapeDtypeStruct((quarter, 2 * rows), jnp.float32)
    message = jax.ShapeDtypeStruct((16, quarter, 2 * rows + 64), jnp.bfloat16)
    half_gram = jax.ShapeDtypeStruct((16 * rows, rows), jnp.bfloat16)
    columns_seen = pltpu.VMEM((16 * rows, half_cols), jnp.float32)
    gram_high, gram_low, sent = pl.pallas_call(
        split_kernel,
        out_shape=(half_gram, half_gram, message),
        in_specs=[smem, vmem, vmem],
        out_specs=(vmem, vmem, vmem),
        compiler_params=params,
    )(place, gram, target)
    got = lax.all_to_all(sent, FEAT, 0, 0)
    transform, update, sent, scalars = pl.pallas_call(
        functools.partial(first_kernel, token_total, order_all),
        out_shape=(tile, tile, message, jax.ShapeDtypeStruct((8, 128), jnp.float32)),
        in_specs=[smem] + [vmem] * 4,
        out_specs=(vmem,) * 4,
        scratch_shapes=[columns_seen],
        compiler_params=params,
    )(place, got, gram_high, gram_low, target)
    got = lax.all_to_all(sent, FEAT, 0, 0)
    return pl.pallas_call(
        functools.partial(second_kernel, token_total),
        out_shape=jax.ShapeDtypeStruct((rows, half_cols), jnp.float32),
        in_specs=[smem] + [vmem] * 7,
        out_specs=vmem,
        scratch_shapes=[columns_seen],
        compiler_params=params,
    )(place, got, gram_high, gram_low, target, transform, update, scalars)


def solution(mesh):
    fine = Mesh(mesh.devices.reshape(SIZES), ALL)
    spec = P(FEAT, TOK)
    return jax.shard_map(
        body, mesh=fine, in_specs=(spec, spec), out_specs=spec, check_vma=False
    )
```

```python
import functools

import jax
import jax.numpy as jnp
from jax import lax
from jax.experimental import pallas as pl
from jax.experimental.pallas import tpu as pltpu
from jax.sharding import Mesh, PartitionSpec as P

ITERS = 2
ridge_share = 0.2
TOK = ("yh", "x", "c")
FEAT = ("yl", "z")
ALL = TOK + FEAT
SIZES = (4, 4, 2, 2, 8)


def shift(array, axis, size, step):
    return lax.ppermute(array, axis, [(i, (i + step) % size) for i in range(size)])


def spread(array, axes, count):
    return lax.all_to_all(
        jnp.broadcast_to(array[None], (count,) + array.shape), axes, 0, 0
    )


def tile_moves(flip):
    moves = []
    for yh in range(4):
        for x in range(4):
            for c in range(2):
                for yl in range(2):
                    for z in range(8):
                        other_yl, half = yh // 2, yh % 2
                        source = (((yh * 4 + x) * 2 + c) * 2 + yl) * 8 + z
                        to_yl = (x % 2) ^ flip
                        to_z = (z + 7 + 4 * yl + 2 * c + x // 2) % 8
                        to_yh, to_x = other_yl * 2 + z // 4, z % 4
                        target = (((to_yh * 4 + to_x) * 2 + half) * 2 + to_yl) * 8 + to_z
                        moves.append((source, target))
    return moves


def round_half(array):
    return array.astype(jnp.bfloat16).astype(jnp.float32)


def pack_kernel(early, late, packed):
    rows, quarter, half_cols = 160, 40, 80
    sums = [(part[0] + part[1]) + (part[2] + part[3]) for part in (early, late)]
    for to_yh in range(4):
        gram_from, top = sums[to_yh // 2], quarter * (to_yh % 2)
        left = 2 * rows + half_cols * to_yh
        for to_yl in range(2):
            to = 2 * to_yh + to_yl
            packed[to, :, :rows] = gram_from[
                top : top + quarter, rows * to_yl : rows * (to_yl + 1)
            ]
            for n in range(2):
                at = rows + half_cols * n
                packed[to, :, at : at + half_cols] = sums[to_yl][
                    quarter * n : quarter * (n + 1), left : left + half_cols
                ]


def split_kernel(place, gram, target, high_out, low_out, sent):
    yl = place[0]
    rows, quarter = 160, 40
    sums = jnp.zeros((1, rows), jnp.float32)
    trace = jnp.zeros((1, 1), jnp.float32)
    at_row = lax.broadcasted_iota(jnp.int32, (quarter, rows), 0)
    at_col = lax.broadcasted_iota(jnp.int32, (quarter, rows), 1)
    for q in range(4):
        for k in range(2):
            n = q * 2 + k
            block = gram[:, :, n * rows : (n + 1) * rows].reshape(2 * rows, rows)
            sums += jnp.sum(jnp.abs(block), 0, keepdims=True)
            if q < 2:
                for m in range(2):
                    own = block[(2 + m) * quarter : (3 + m) * quarter]
                    on_diagonal = (at_col == at_row + 80 * m + quarter * q) & (yl == k)
                    trace += jnp.sum(jnp.where(on_diagonal, own, 0.0), keepdims=True)
            high = block.astype(jnp.bfloat16)
            high_out[n * 2 * rows : (n + 1) * 2 * rows, :] = high
            low_out[n * 2 * rows : (n + 1) * 2 * rows, :] = (
                block - high.astype(jnp.float32)
            ).astype(jnp.bfloat16)
    peak = jnp.max(sums, keepdims=True)
    lane = lax.broadcasted_iota(jnp.int32, (quarter, 64), 1)
    value = jnp.where(lane < 3, peak, trace)
    first = round_half(value)
    second = round_half(value - first)
    third = value - first - second
    which = lane % 3
    tail = jnp.where(which == 0, first, jnp.where(which == 1, second, third))
    body_half = target[...].astype(jnp.bfloat16)
    tail_half = tail.astype(jnp.bfloat16)
    for d in range(16):
        sent[d, :, : 2 * rows] = body_half
        sent[d, :, 2 * rows :] = tail_half


def times_gram(z, got, high, low, seen):
    rows, quarter, half_cols = 160, 40, 80
    for k in range(2):
        for s in range(8):
            p, c, l = s // 4, s // 2 % 2, s % 2
            block = got[8 * k + lax.rem(z + 7 + s, 8)].astype(jnp.float32)
            for m in range(2):
                for a in range(2):
                    g = 2 * m + a
                    top = ((2 * p + a) * 2 + k) * 2 * rows + (4 * c + 2 * l + m) * quarter
                    seen[top : top + quarter, :] = block[:, g * half_cols : (g + 1) * half_cols]
    side = seen[...].astype(jnp.bfloat16)
    product = 0.0
    for part in (high, low):
        product += lax.dot_general(
            part[...], side, (((0,), (0,)), ((), ())), preferred_element_type=jnp.float32
        )
    return jnp.concatenate([product[quarter * g : quarter * (g + 1)] for g in range(4)], 1)


def first_kernel(
    token_total, order_all, place, got, high, low, target_in, transform_out, update_out,
    sent, scalars, seen,
):
    rows = 160
    applied = times_gram(place[1], got, high, low, seen) / token_total
    peak_all = energy = None
    for d in range(16):
        tail = got[d][:, 2 * rows :].astype(jnp.float32)[:1]
        peak = tail[:, 0:1] + tail[:, 1:2] + tail[:, 2:3]
        trace = tail[:, 3:4] + tail[:, 4:5] + tail[:, 5:6]
        peak_all = peak if d == 0 else jnp.maximum(peak_all, peak)
        energy = trace if d == 0 else energy + trace
    ridge_term = ridge_share * energy / (token_total * order_all)
    upper_bound = peak_all / token_total + ridge_term
    center = (upper_bound + ridge_term) / 2.0
    half_span = (upper_bound - ridge_term) / 2.0
    ratio_now = half_span / center
    ratio_next = 1.0 / (2.0 * center / half_span - ratio_now)
    target = target_in[...]
    start = target / center
    residual = target - (applied + ridge_term * round_half(target)) / center
    update = ratio_next * ratio_now * start + 2.0 * ratio_next / half_span * residual
    transform = start + update
    ratio_last = 1.0 / (2.0 * center / half_span - ratio_next)
    transform_out[...] = transform
    update_out[...] = update
    lane = lax.broadcasted_iota(jnp.int32, (8, 128), 1)
    scalars[...] = jnp.where(
        lane == 0,
        ridge_term,
        jnp.where(lane == 1, ratio_last * ratio_next, 2.0 * ratio_last / half_span),
    )
    half = transform.astype(jnp.bfloat16)
    for d in range(16):
        sent[d, :, : 2 * rows] = half
        sent[d, :, 2 * rows :] = jnp.zeros((40, 64), jnp.bfloat16)


def second_kernel(
    token_total, place, got, high, low, target_in, transform_in, update_in, scalars, out, seen
):
    quarter, half_cols = 40, 80
    applied = times_gram(place[1], got, high, low, seen) / token_total
    ridge_term, keep, gain = scalars[0:1, 0:1], scalars[0:1, 1:2], scalars[0:1, 2:3]
    transform = transform_in[...]
    residual = target_in[...] - (applied + ridge_term * round_half(transform))
    final = transform + (keep * update_in[...] + gain * residual)
    for g in range(4):
        out[quarter * g : quarter * (g + 1), :] = final[:, half_cols * g : half_cols * (g + 1)]


def body(entering, leaving):
    yl = lax.axis_index("yl")
    z = lax.axis_index("z")
    rows = entering.shape[0]
    quarter = rows // 4
    half_cols = rows // 2
    token_total = entering.shape[1] * 32
    order_all = rows * 16
    low = yl == 0

    pair = jnp.concatenate([entering, leaving], 0)
    other = shift(pair, "yl", 2, 1)
    first = jnp.where(low, pair, other)
    second = jnp.where(low, other, pair)
    columns = jnp.concatenate([first[:rows], second[:rows], first[rows:], second[rows:]], 0)

    def products(blocks, order):
        whole = jnp.zeros((len(blocks), rows, 4 * rows), jnp.float32)
        for n in order:
            product = lax.dot_general(
                blocks[n], columns, (((1,), (1,)), ((), ())), preferred_element_type=jnp.float32
            )
            whole = lax.dynamic_update_index_in_dim(whole, product, n, 0)
        return whole

    def core_sum(array):
        array = lax.all_to_all(array.reshape(2, 2, rows, 4 * rows), "c", 0, 0)
        return jnp.sum(array, 0).reshape(4, half_cols, 4 * rows)

    down_1, up_1 = shift(entering, "z", 8, -1), shift(entering, "z", 8, 1)
    down_2, up_2 = shift(down_1, "z", 8, -1), shift(up_1, "z", 8, 1)
    down_3 = shift(down_2, "z", 8, -1)
    early = products([up_1, entering, down_1, down_2], (1, 0, 2, 3))
    early, down_3, up_2 = lax.optimization_barrier((early, down_3, up_2))
    down_4, up_3 = shift(down_3, "z", 8, -1), shift(up_2, "z", 8, 1)
    early = lax.all_to_all(core_sum(early), "x", 0, 0)
    late = products([down_3, down_4, up_3, up_2], (0, 3, 1, 2))
    early, late = lax.optimization_barrier((early, late))
    late = lax.all_to_all(core_sum(late), "x", 0, 0)
    packed = pl.pallas_call(
        pack_kernel,
        out_shape=jax.ShapeDtypeStruct((8, quarter, 2 * rows), jnp.float32),
        in_specs=[pl.BlockSpec(memory_space=pltpu.VMEM)] * 2,
        out_specs=pl.BlockSpec(memory_space=pltpu.VMEM),
        compiler_params=pltpu.CompilerParams(vmem_limit_bytes=40 * 2**20),
    )(early, late)
    own = lax.all_to_all(packed, ("yh", "yl"), 0, 0)
    own = jnp.sum(own.reshape(4, 2, quarter, 2 * rows), 0)

    even = (lax.axis_index("x") & 1) == 0
    near = jnp.where(even, own[0, :, rows:], own[1, :, rows:])
    far = jnp.where(even, own[1, :, rows:], own[0, :, rows:])
    near = lax.ppermute(near, ALL, tile_moves(0))
    far = lax.ppermute(far, ALL, tile_moves(1))
    gram_part = jnp.concatenate([own[0, :, :rows], own[1, :, :rows]], 1)
    gram_part = spread(gram_part, "yh", 4)
    gram_part, near, far = lax.optimization_barrier((gram_part, near, far))
    target = (
        jnp.concatenate([jnp.where(low, near, far), jnp.where(low, far, near)], 1) / token_total
    )
    gram_part = jnp.concatenate([gram_part[q] for q in range(4)], 1)
    gram_part = spread(gram_part, "x", 4)
    gram = spread(gram_part, "c", 2).reshape(8, quarter, 8 * rows)

    place = jnp.stack([yl, z]).astype(jnp.int32)
    vmem = pl.BlockSpec(memory_space=pltpu.VMEM)
    smem = pl.BlockSpec(memory_space=pltpu.SMEM)
    params = pltpu.CompilerParams(vmem_limit_bytes=40 * 2**20)
    tile = jax.ShapeDtypeStruct((quarter, 2 * rows), jnp.float32)
    message = jax.ShapeDtypeStruct((16, quarter, 2 * rows + 64), jnp.bfloat16)
    half_gram = jax.ShapeDtypeStruct((16 * rows, rows), jnp.bfloat16)
    columns_seen = pltpu.VMEM((16 * rows, half_cols), jnp.float32)
    gram_high, gram_low, sent = pl.pallas_call(
        split_kernel,
        out_shape=(half_gram, half_gram, message),
        in_specs=[smem, vmem, vmem],
        out_specs=(vmem, vmem, vmem),
        compiler_params=params,
    )(place, gram, target)
    got = lax.all_to_all(sent, FEAT, 0, 0)
    transform, update, sent, scalars = pl.pallas_call(
        functools.partial(first_kernel, token_total, order_all),
        out_shape=(tile, tile, message, jax.ShapeDtypeStruct((8, 128), jnp.float32)),
        in_specs=[smem] + [vmem] * 4,
        out_specs=(vmem,) * 4,
        scratch_shapes=[columns_seen],
        compiler_params=params,
    )(place, got, gram_high, gram_low, target)
    got = lax.all_to_all(sent, FEAT, 0, 0)
    return pl.pallas_call(
        functools.partial(second_kernel, token_total),
        out_shape=jax.ShapeDtypeStruct((rows, half_cols), jnp.float32),
        in_specs=[smem] + [vmem] * 7,
        out_specs=vmem,
        scratch_shapes=[columns_seen],
        compiler_params=params,
    )(place, got, gram_high, gram_low, target, transform, update, scalars)


def solution(mesh):
    fine = Mesh(mesh.devices.reshape(SIZES), ALL)
    spec = P(FEAT, TOK)
    return jax.shard_map(
        body, mesh=fine, in_specs=(spec, spec), out_specs=spec, check_vma=False
    )
```

```python
import functools

import jax
import jax.numpy as jnp
from jax import lax
from jax.experimental import pallas as pl
from jax.experimental.pallas import tpu as pltpu
from jax.sharding import Mesh, PartitionSpec as P

ITERS = 2
ridge_share = 0.2
TOK = ("yh", "x", "c")
FEAT = ("yl", "z")
ALL = TOK + FEAT
SIZES = (4, 4, 2, 2, 8)
OFFSETS = (7, 6, 5, 4, 0, 1, 2, 3)


def shift(array, axis, size, step):
    return lax.ppermute(array, axis, [(i, (i + step) % size) for i in range(size)])


def spread(array, axes, count):
    return lax.all_to_all(
        jnp.broadcast_to(array[None], (count,) + array.shape), axes, 0, 0
    )


def tile_moves():
    moves = []
    for yh in range(4):
        for x in range(4):
            for c in range(2):
                for yl in range(2):
                    for z in range(8):
                        other_yl, half = yh // 2, yh % 2
                        source = (((yh * 4 + x) * 2 + c) * 2 + yl) * 8 + z
                        to_z = (z + OFFSETS[4 * c + x]) % 8
                        to_yh, to_x = other_yl * 2 + z // 4, z % 4
                        target = (((to_yh * 4 + to_x) * 2 + half) * 2 + yl) * 8 + to_z
                        moves.append((source, target))
    return moves


def round_half(array):
    return array.astype(jnp.bfloat16).astype(jnp.float32)


def split_kernel(place, gram, target, high_out, low_out, sent):
    yl = place[0]
    rows, quarter = 160, 40
    sums = jnp.zeros((1, rows), jnp.float32)
    trace = jnp.zeros((1, 1), jnp.float32)
    at_row = lax.broadcasted_iota(jnp.int32, (quarter, rows), 0)
    at_col = lax.broadcasted_iota(jnp.int32, (quarter, rows), 1)
    for q in range(4):
        for k in range(2):
            n = q * 2 + k
            block = gram[:, :, n * rows : (n + 1) * rows].reshape(2 * rows, rows)
            sums += jnp.sum(jnp.abs(block), 0, keepdims=True)
            on_diagonal = (at_col == at_row + quarter * q) & (yl == k)
            own = block[4 * quarter : 5 * quarter]
            trace += jnp.sum(jnp.where(on_diagonal, own, 0.0), keepdims=True)
            high = block.astype(jnp.bfloat16)
            high_out[n * 2 * rows : (n + 1) * 2 * rows, :] = high
            low_out[n * 2 * rows : (n + 1) * 2 * rows, :] = (
                block - high.astype(jnp.float32)
            ).astype(jnp.bfloat16)
    peak = jnp.max(sums, keepdims=True)
    lane = lax.broadcasted_iota(jnp.int32, (quarter, 64), 1)
    value = jnp.where(lane < 3, peak, trace)
    first = round_half(value)
    second = round_half(value - first)
    third = value - first - second
    which = lane % 3
    tail = jnp.where(which == 0, first, jnp.where(which == 1, second, third))
    body_half = target[...].astype(jnp.bfloat16)
    tail_half = tail.astype(jnp.bfloat16)
    for d in range(16):
        sent[d, :, : 2 * rows] = body_half
        sent[d, :, 2 * rows :] = tail_half


def times_gram(z, got, high, low, seen):
    rows, quarter, half_cols = 160, 40, 80
    for k in range(2):
        for s in range(8):
            block = got[8 * k + lax.rem(z + OFFSETS[s], 8)].astype(jnp.float32)
            for q in range(4):
                top = (q * 2 + k) * 2 * rows + s * quarter
                seen[top : top + quarter, :] = block[:, q * half_cols : (q + 1) * half_cols]
    side = seen[...].astype(jnp.bfloat16)
    product = 0.0
    for part in (high, low):
        product += lax.dot_general(
            part[...], side, (((0,), (0,)), ((), ())), preferred_element_type=jnp.float32
        )
    return jnp.concatenate([product[quarter * g : quarter * (g + 1)] for g in range(4)], 1)


def first_kernel(
    token_total, order_all, place, got, high, low, target_in, transform_out, update_out,
    sent, scalars, seen,
):
    rows = 160
    applied = times_gram(place[1], got, high, low, seen) / token_total
    peak_all = energy = None
    for d in range(16):
        tail = got[d][:, 2 * rows :].astype(jnp.float32)[:1]
        peak = tail[:, 0:1] + tail[:, 1:2] + tail[:, 2:3]
        trace = tail[:, 3:4] + tail[:, 4:5] + tail[:, 5:6]
        peak_all = peak if d == 0 else jnp.maximum(peak_all, peak)
        energy = trace if d == 0 else energy + trace
    ridge_term = ridge_share * energy / (token_total * order_all)
    upper_bound = peak_all / token_total + ridge_term
    center = (upper_bound + ridge_term) / 2.0
    half_span = (upper_bound - ridge_term) / 2.0
    ratio_now = half_span / center
    ratio_next = 1.0 / (2.0 * center / half_span - ratio_now)
    target = target_in[...]
    start = target / center
    residual = target - (applied + ridge_term * round_half(target)) / center
    update = ratio_next * ratio_now * start + 2.0 * ratio_next / half_span * residual
    transform = start + update
    ratio_last = 1.0 / (2.0 * center / half_span - ratio_next)
    transform_out[...] = transform
    update_out[...] = update
    lane = lax.broadcasted_iota(jnp.int32, (8, 128), 1)
    scalars[...] = jnp.where(
        lane == 0,
        ridge_term,
        jnp.where(lane == 1, ratio_last * ratio_next, 2.0 * ratio_last / half_span),
    )
    half = transform.astype(jnp.bfloat16)
    for d in range(16):
        sent[d, :, : 2 * rows] = half
        sent[d, :, 2 * rows :] = jnp.zeros((40, 64), jnp.bfloat16)


def second_kernel(
    token_total, place, got, high, low, target_in, transform_in, update_in, scalars, out, seen
):
    quarter, half_cols = 40, 80
    applied = times_gram(place[1], got, high, low, seen) / token_total
    ridge_term, keep, gain = scalars[0:1, 0:1], scalars[0:1, 1:2], scalars[0:1, 2:3]
    transform = transform_in[...]
    residual = target_in[...] - (applied + ridge_term * round_half(transform))
    final = transform + (keep * update_in[...] + gain * residual)
    for g in range(4):
        out[quarter * g : quarter * (g + 1), :] = final[:, half_cols * g : half_cols * (g + 1)]


def body(entering, leaving):
    yl = lax.axis_index("yl")
    z = lax.axis_index("z")
    rows = entering.shape[0]
    quarter = rows // 4
    half_cols = rows // 2
    token_total = entering.shape[1] * 32
    order_all = rows * 16
    low = yl == 0

    pair = jnp.concatenate([entering, leaving], 0)
    other = shift(pair, "yl", 2, 1)
    first = jnp.where(low, pair, other)
    second = jnp.where(low, other, pair)
    columns = jnp.concatenate([first[:rows], second[:rows], first[rows:], second[rows:]], 0)

    columns_there = shift(columns, "c", 2, 1)
    first = [(z, (z + 1) % 8) for z in range(8)] + [(8 + z, 8 + z) for z in range(8)]
    later = [(z, (z + 1) % 8) for z in range(8)] + [(8 + z, 8 + (z + 7) % 8) for z in range(8)]
    here, there = entering, shift(entering, "c", 2, 1)
    partial = jnp.zeros((4, rows, 4 * rows), jnp.float32)
    for step in range(4):
        if step == 3:
            here, columns_there = lax.optimization_barrier((here, columns_there))
        here = lax.ppermute(here, ("c", "z"), later if step else first)
        there = lax.ppermute(there, ("c", "z"), later if step else first)
        product = lax.dot_general(
            here, columns, (((1,), (1,)), ((), ())), preferred_element_type=jnp.float32
        ) + lax.dot_general(
            there, columns_there, (((1,), (1,)), ((), ())), preferred_element_type=jnp.float32
        )
        partial = lax.dynamic_update_index_in_dim(partial, product, step, 0)
    partial = jnp.sum(lax.all_to_all(partial, "x", 0, 0), 0)
    packed = []
    for to_yh in range(4):
        for to_yl in range(2):
            top = half_cols * to_yl
            left = 2 * rows + half_cols * to_yh
            packed.append(
                jnp.concatenate(
                    [
                        partial[
                            quarter * to_yh : quarter * (to_yh + 1),
                            rows * to_yl : rows * (to_yl + 1),
                        ],
                        partial[top : top + quarter, left : left + half_cols],
                        partial[top + quarter : top + 2 * quarter, left : left + half_cols],
                    ],
                    1,
                )
            )
    own = lax.all_to_all(jnp.stack(packed), ("yh", "yl"), 0, 0)
    own = jnp.sum(own.reshape(4, 2, quarter, 2 * rows), 0)

    cross_own = jnp.concatenate([own[0, :, rows:], own[1, :, rows:]], 1)
    cross_own = lax.ppermute(cross_own, ALL, tile_moves())
    cross_swap = shift(cross_own, "yl", 2, 1)
    target = jnp.where(
        low,
        jnp.concatenate([cross_own[:, :rows], cross_swap[:, :rows]], 1),
        jnp.concatenate([cross_swap[:, rows:], cross_own[:, rows:]], 1),
    ) / token_total

    gram_part = jnp.concatenate([own[0, :, :rows], own[1, :, :rows]], 1)
    gram_part = spread(gram_part, "yh", 4)
    gram_part = jnp.concatenate([gram_part[q] for q in range(4)], 1)
    gram_part = spread(gram_part, "x", 4)
    gram = spread(gram_part, "c", 2).reshape(8, quarter, 8 * rows)

    place = jnp.stack([yl, z]).astype(jnp.int32)
    vmem = pl.BlockSpec(memory_space=pltpu.VMEM)
    smem = pl.BlockSpec(memory_space=pltpu.SMEM)
    params = pltpu.CompilerParams(vmem_limit_bytes=40 * 2**20)
    tile = jax.ShapeDtypeStruct((quarter, 2 * rows), jnp.float32)
    message = jax.ShapeDtypeStruct((16, quarter, 2 * rows + 64), jnp.bfloat16)
    half_gram = jax.ShapeDtypeStruct((16 * rows, rows), jnp.bfloat16)
    columns_seen = pltpu.VMEM((16 * rows, half_cols), jnp.float32)
    gram_high, gram_low, sent = pl.pallas_call(
        split_kernel,
        out_shape=(half_gram, half_gram, message),
        in_specs=[smem, vmem, vmem],
        out_specs=(vmem, vmem, vmem),
        compiler_params=params,
    )(place, gram, target)
    got = lax.all_to_all(sent, FEAT, 0, 0)
    transform, update, sent, scalars = pl.pallas_call(
        functools.partial(first_kernel, token_total, order_all),
        out_shape=(tile, tile, message, jax.ShapeDtypeStruct((8, 128), jnp.float32)),
        in_specs=[smem] + [vmem] * 4,
        out_specs=(vmem,) * 4,
        scratch_shapes=[columns_seen],
        compiler_params=params,
    )(place, got, gram_high, gram_low, target)
    got = lax.all_to_all(sent, FEAT, 0, 0)
    return pl.pallas_call(
        functools.partial(second_kernel, token_total),
        out_shape=jax.ShapeDtypeStruct((rows, half_cols), jnp.float32),
        in_specs=[smem] + [vmem] * 7,
        out_specs=vmem,
        scratch_shapes=[columns_seen],
        compiler_params=params,
    )(place, got, gram_high, gram_low, target, transform, update, scalars)


def solution(mesh):
    fine = Mesh(mesh.devices.reshape(SIZES), ALL)
    spec = P(FEAT, TOK)
    return jax.shard_map(
        body, mesh=fine, in_specs=(spec, spec), out_specs=spec, check_vma=False
    )
```

```python
import functools

import jax
import jax.numpy as jnp
from jax import lax
from jax.experimental import pallas as pl
from jax.experimental.pallas import tpu as pltpu
from jax.sharding import Mesh, PartitionSpec as P

ITERS = 2
ridge_share = 0.2
TOK = ("yh", "x", "c")
FEAT = ("yl", "z")
ALL = TOK + FEAT
SIZES = (4, 4, 2, 2, 8)
OFFSETS = (7, 6, 5, 4, 0, 1, 2, 3)


def shift(array, axis, size, step):
    return lax.ppermute(array, axis, [(i, (i + step) % size) for i in range(size)])


def spread(array, axes, count):
    return lax.all_to_all(
        jnp.broadcast_to(array[None], (count,) + array.shape), axes, 0, 0
    )


def tile_moves():
    moves = []
    for yh in range(4):
        for x in range(4):
            for c in range(2):
                for yl in range(2):
                    for z in range(8):
                        other_yl, half = yh // 2, yh % 2
                        source = (((yh * 4 + x) * 2 + c) * 2 + yl) * 8 + z
                        to_z = (z + OFFSETS[4 * c + x]) % 8
                        to_yh, to_x = other_yl * 2 + z // 4, z % 4
                        target = (((to_yh * 4 + to_x) * 2 + half) * 2 + yl) * 8 + to_z
                        moves.append((source, target))
    return moves


def round_half(array):
    return array.astype(jnp.bfloat16).astype(jnp.float32)


def split_kernel(place, gram, target, high_out, low_out, sent):
    yl = place[0]
    rows, quarter = 160, 40
    sums = jnp.zeros((1, rows), jnp.float32)
    trace = jnp.zeros((1, 1), jnp.float32)
    at_row = lax.broadcasted_iota(jnp.int32, (quarter, rows), 0)
    at_col = lax.broadcasted_iota(jnp.int32, (quarter, rows), 1)
    for q in range(4):
        for k in range(2):
            n = q * 2 + k
            block = gram[:, :, n * rows : (n + 1) * rows].reshape(2 * rows, rows)
            sums += jnp.sum(jnp.abs(block), 0, keepdims=True)
            on_diagonal = (at_col == at_row + quarter * q) & (yl == k)
            own = block[4 * quarter : 5 * quarter]
            trace += jnp.sum(jnp.where(on_diagonal, own, 0.0), keepdims=True)
            high = block.astype(jnp.bfloat16)
            high_out[n * 2 * rows : (n + 1) * 2 * rows, :] = high
            low_out[n * 2 * rows : (n + 1) * 2 * rows, :] = (
                block - high.astype(jnp.float32)
            ).astype(jnp.bfloat16)
    peak = jnp.max(sums, keepdims=True)
    lane = lax.broadcasted_iota(jnp.int32, (quarter, 64), 1)
    value = jnp.where(lane < 3, peak, trace)
    first = round_half(value)
    second = round_half(value - first)
    third = value - first - second
    which = lane % 3
    tail = jnp.where(which == 0, first, jnp.where(which == 1, second, third))
    body_half = target[...].astype(jnp.bfloat16)
    tail_half = tail.astype(jnp.bfloat16)
    for d in range(16):
        sent[d, :, : 2 * rows] = body_half
        sent[d, :, 2 * rows :] = tail_half


def times_gram(z, got, high, low, seen):
    rows, quarter, half_cols = 160, 40, 80
    for k in range(2):
        for s in range(8):
            block = got[8 * k + lax.rem(z + OFFSETS[s], 8)].astype(jnp.float32)
            for q in range(4):
                top = (q * 2 + k) * 2 * rows + s * quarter
                seen[top : top + quarter, :] = block[:, q * half_cols : (q + 1) * half_cols]
    side = seen[...].astype(jnp.bfloat16)
    product = 0.0
    for part in (high, low):
        product += lax.dot_general(
            part[...], side, (((0,), (0,)), ((), ())), preferred_element_type=jnp.float32
        )
    return jnp.concatenate([product[quarter * g : quarter * (g + 1)] for g in range(4)], 1)


def first_kernel(
    token_total, order_all, place, got, high, low, target_in, transform_out, update_out,
    sent, scalars, seen,
):
    rows = 160
    applied = times_gram(place[1], got, high, low, seen) / token_total
    peak_all = energy = None
    for d in range(16):
        tail = got[d][:, 2 * rows :].astype(jnp.float32)[:1]
        peak = tail[:, 0:1] + tail[:, 1:2] + tail[:, 2:3]
        trace = tail[:, 3:4] + tail[:, 4:5] + tail[:, 5:6]
        peak_all = peak if d == 0 else jnp.maximum(peak_all, peak)
        energy = trace if d == 0 else energy + trace
    ridge_term = ridge_share * energy / (token_total * order_all)
    upper_bound = peak_all / token_total + ridge_term
    center = (upper_bound + ridge_term) / 2.0
    half_span = (upper_bound - ridge_term) / 2.0
    ratio_now = half_span / center
    ratio_next = 1.0 / (2.0 * center / half_span - ratio_now)
    target = target_in[...]
    start = target / center
    residual = target - (applied + ridge_term * round_half(target)) / center
    update = ratio_next * ratio_now * start + 2.0 * ratio_next / half_span * residual
    transform = start + update
    ratio_last = 1.0 / (2.0 * center / half_span - ratio_next)
    transform_out[...] = transform
    update_out[...] = update
    lane = lax.broadcasted_iota(jnp.int32, (8, 128), 1)
    scalars[...] = jnp.where(
        lane == 0,
        ridge_term,
        jnp.where(lane == 1, ratio_last * ratio_next, 2.0 * ratio_last / half_span),
    )
    half = transform.astype(jnp.bfloat16)
    for d in range(16):
        sent[d, :, : 2 * rows] = half
        sent[d, :, 2 * rows :] = jnp.zeros((40, 64), jnp.bfloat16)


def second_kernel(
    token_total, place, got, high, low, target_in, transform_in, update_in, scalars, out, seen
):
    quarter, half_cols = 40, 80
    applied = times_gram(place[1], got, high, low, seen) / token_total
    ridge_term, keep, gain = scalars[0:1, 0:1], scalars[0:1, 1:2], scalars[0:1, 2:3]
    transform = transform_in[...]
    residual = target_in[...] - (applied + ridge_term * round_half(transform))
    final = transform + (keep * update_in[...] + gain * residual)
    for g in range(4):
        out[quarter * g : quarter * (g + 1), :] = final[:, half_cols * g : half_cols * (g + 1)]


def body(entering, leaving):
    yl = lax.axis_index("yl")
    z = lax.axis_index("z")
    rows = entering.shape[0]
    quarter = rows // 4
    half_cols = rows // 2
    token_total = entering.shape[1] * 32
    order_all = rows * 16
    low = yl == 0

    first = [(z, (z + 1) % 8) for z in range(8)] + [(8 + z, 8 + z) for z in range(8)]
    later = [(z, (z + 1) % 8) for z in range(8)] + [(8 + z, 8 + (z + 7) % 8) for z in range(8)]
    here, there = [lax.ppermute(entering, ("c", "z"), first)], []
    swapped, entering, leaving = lax.optimization_barrier(
        (shift(entering, "c", 2, 1), entering, leaving)
    )
    there.append(lax.ppermute(swapped, ("c", "z"), first))
    pair = jnp.concatenate([entering, leaving], 0)
    other = shift(pair, "yl", 2, 1)
    here[0], there[0] = lax.optimization_barrier((here[0], there[0]))
    here.append(lax.ppermute(here[0], ("c", "z"), later))
    there.append(lax.ppermute(there[0], ("c", "z"), later))
    here[1], there[1], other = lax.optimization_barrier((here[1], there[1], other))
    columns = jnp.concatenate(
        [
            jnp.where(low, pair[:rows], other[:rows]),
            jnp.where(low, other[:rows], pair[:rows]),
            jnp.where(low, pair[rows:], other[rows:]),
            jnp.where(low, other[rows:], pair[rows:]),
        ],
        0,
    )
    columns_there = shift(columns, "c", 2, 1)
    here.append(lax.ppermute(here[1], ("c", "z"), later))
    there.append(lax.ppermute(there[1], ("c", "z"), later))
    here[2], there[2], columns_there = lax.optimization_barrier(
        (here[2], there[2], columns_there)
    )
    here.append(lax.ppermute(here[2], ("c", "z"), later))
    there.append(lax.ppermute(there[2], ("c", "z"), later))
    partial = jnp.zeros((4, rows, 4 * rows), jnp.float32)
    for step in range(4):
        product = lax.dot_general(
            here[step], columns, (((1,), (1,)), ((), ())), preferred_element_type=jnp.float32
        ) + lax.dot_general(
            there[step], columns_there, (((1,), (1,)), ((), ())), preferred_element_type=jnp.float32
        )
        partial = lax.dynamic_update_index_in_dim(partial, product, step, 0)
    partial = jnp.sum(lax.all_to_all(partial, "x", 0, 0), 0)
    packed = []
    for to_yh in range(4):
        for to_yl in range(2):
            top = half_cols * to_yl
            left = 2 * rows + half_cols * to_yh
            packed.append(
                jnp.concatenate(
                    [
                        partial[
                            quarter * to_yh : quarter * (to_yh + 1),
                            rows * to_yl : rows * (to_yl + 1),
                        ],
                        partial[top : top + quarter, left : left + half_cols],
                        partial[top + quarter : top + 2 * quarter, left : left + half_cols],
                    ],
                    1,
                )
            )
    own = lax.all_to_all(jnp.stack(packed), ("yh", "yl"), 0, 0)
    own = jnp.sum(own.reshape(4, 2, quarter, 2 * rows), 0)

    cross_own = jnp.concatenate([own[0, :, rows:], own[1, :, rows:]], 1)
    cross_own = lax.ppermute(cross_own, ALL, tile_moves())
    cross_swap = shift(cross_own, "yl", 2, 1)
    target = jnp.where(
        low,
        jnp.concatenate([cross_own[:, :rows], cross_swap[:, :rows]], 1),
        jnp.concatenate([cross_swap[:, rows:], cross_own[:, rows:]], 1),
    ) / token_total

    gram_part = jnp.concatenate([own[0, :, :rows], own[1, :, :rows]], 1)
    gram_part = spread(gram_part, "yh", 4)
    gram_part = jnp.concatenate([gram_part[q] for q in range(4)], 1)
    gram_part = spread(gram_part, "x", 4)
    gram = spread(gram_part, "c", 2).reshape(8, quarter, 8 * rows)

    place = jnp.stack([yl, z]).astype(jnp.int32)
    vmem = pl.BlockSpec(memory_space=pltpu.VMEM)
    smem = pl.BlockSpec(memory_space=pltpu.SMEM)
    params = pltpu.CompilerParams(vmem_limit_bytes=40 * 2**20)
    tile = jax.ShapeDtypeStruct((quarter, 2 * rows), jnp.float32)
    message = jax.ShapeDtypeStruct((16, quarter, 2 * rows + 64), jnp.bfloat16)
    half_gram = jax.ShapeDtypeStruct((16 * rows, rows), jnp.bfloat16)
    columns_seen = pltpu.VMEM((16 * rows, half_cols), jnp.float32)
    gram_high, gram_low, sent = pl.pallas_call(
        split_kernel,
        out_shape=(half_gram, half_gram, message),
        in_specs=[smem, vmem, vmem],
        out_specs=(vmem, vmem, vmem),
        compiler_params=params,
    )(place, gram, target)
    got = lax.all_to_all(sent, FEAT, 0, 0)
    transform, update, sent, scalars = pl.pallas_call(
        functools.partial(first_kernel, token_total, order_all),
        out_shape=(tile, tile, message, jax.ShapeDtypeStruct((8, 128), jnp.float32)),
        in_specs=[smem] + [vmem] * 4,
        out_specs=(vmem,) * 4,
        scratch_shapes=[columns_seen],
        compiler_params=params,
    )(place, got, gram_high, gram_low, target)
    got = lax.all_to_all(sent, FEAT, 0, 0)
    return pl.pallas_call(
        functools.partial(second_kernel, token_total),
        out_shape=jax.ShapeDtypeStruct((rows, half_cols), jnp.float32),
        in_specs=[smem] + [vmem] * 7,
        out_specs=vmem,
        scratch_shapes=[columns_seen],
        compiler_params=params,
    )(place, got, gram_high, gram_low, target, transform, update, scalars)


def solution(mesh):
    fine = Mesh(mesh.devices.reshape(SIZES), ALL)
    spec = P(FEAT, TOK)
    return jax.shard_map(
        body, mesh=fine, in_specs=(spec, spec), out_specs=spec, check_vma=False
    )
```

```python
import functools

import jax
import jax.numpy as jnp
from jax import lax
from jax.experimental import pallas as pl
from jax.experimental.pallas import tpu as pltpu
from jax.sharding import Mesh, PartitionSpec as P

ITERS = 2
ridge_share = 0.2
TOK = ("yh", "x", "c")
FEAT = ("yl", "z")
ALL = TOK + FEAT
SIZES = (4, 4, 2, 2, 8)
OFFSETS = (7, 6, 5, 4, 0, 1, 2, 3)


def shift(array, axis, size, step):
    return lax.ppermute(array, axis, [(i, (i + step) % size) for i in range(size)])


def spread(array, axes, count):
    return lax.all_to_all(
        jnp.broadcast_to(array[None], (count,) + array.shape), axes, 0, 0
    )


def tile_moves():
    moves = []
    for yh in range(4):
        for x in range(4):
            for c in range(2):
                for yl in range(2):
                    for z in range(8):
                        other_yl, half = yh // 2, yh % 2
                        source = (((yh * 4 + x) * 2 + c) * 2 + yl) * 8 + z
                        to_z = (z + OFFSETS[4 * c + x]) % 8
                        to_yh, to_x = other_yl * 2 + z // 4, z % 4
                        target = (((to_yh * 4 + to_x) * 2 + half) * 2 + yl) * 8 + to_z
                        moves.append((source, target))
    return moves


def round_half(array):
    return array.astype(jnp.bfloat16).astype(jnp.float32)


def split_kernel(place, gram, target, high_out, low_out, sent):
    yl = place[0]
    rows, quarter = 160, 40
    sums = jnp.zeros((1, rows), jnp.float32)
    trace = jnp.zeros((1, 1), jnp.float32)
    at_row = lax.broadcasted_iota(jnp.int32, (quarter, rows), 0)
    at_col = lax.broadcasted_iota(jnp.int32, (quarter, rows), 1)
    for q in range(4):
        for k in range(2):
            n = q * 2 + k
            block = gram[:, :, n * rows : (n + 1) * rows].reshape(2 * rows, rows)
            sums += jnp.sum(jnp.abs(block), 0, keepdims=True)
            on_diagonal = (at_col == at_row + quarter * q) & (yl == k)
            own = block[4 * quarter : 5 * quarter]
            trace += jnp.sum(jnp.where(on_diagonal, own, 0.0), keepdims=True)
            high = block.astype(jnp.bfloat16)
            high_out[n * 2 * rows : (n + 1) * 2 * rows, :] = high
            low_out[n * 2 * rows : (n + 1) * 2 * rows, :] = (
                block - high.astype(jnp.float32)
            ).astype(jnp.bfloat16)
    peak = jnp.max(sums, keepdims=True)
    lane = lax.broadcasted_iota(jnp.int32, (quarter, 64), 1)
    value = jnp.where(lane < 3, peak, trace)
    first = round_half(value)
    second = round_half(value - first)
    third = value - first - second
    which = lane % 3
    tail = jnp.where(which == 0, first, jnp.where(which == 1, second, third))
    body_half = target[...].astype(jnp.bfloat16)
    tail_half = tail.astype(jnp.bfloat16)
    for d in range(16):
        sent[d, :, : 2 * rows] = body_half
        sent[d, :, 2 * rows :] = tail_half


def times_gram(z, got, high, low, seen):
    rows, quarter, half_cols = 160, 40, 80
    for k in range(2):
        for s in range(8):
            block = got[8 * k + lax.rem(z + OFFSETS[s], 8)].astype(jnp.float32)
            for q in range(4):
                top = (q * 2 + k) * 2 * rows + s * quarter
                seen[top : top + quarter, :] = block[:, q * half_cols : (q + 1) * half_cols]
    side = seen[...].astype(jnp.bfloat16)
    product = 0.0
    for part in (high, low):
        product += lax.dot_general(
            part[...], side, (((0,), (0,)), ((), ())), preferred_element_type=jnp.float32
        )
    return jnp.concatenate([product[quarter * g : quarter * (g + 1)] for g in range(4)], 1)


def first_kernel(
    token_total, order_all, place, got, high, low, target_in, transform_out, update_out,
    sent, scalars, seen,
):
    rows = 160
    applied = times_gram(place[1], got, high, low, seen) / token_total
    peak_all = energy = None
    for d in range(16):
        tail = got[d][:, 2 * rows :].astype(jnp.float32)[:1]
        peak = tail[:, 0:1] + tail[:, 1:2] + tail[:, 2:3]
        trace = tail[:, 3:4] + tail[:, 4:5] + tail[:, 5:6]
        peak_all = peak if d == 0 else jnp.maximum(peak_all, peak)
        energy = trace if d == 0 else energy + trace
    ridge_term = ridge_share * energy / (token_total * order_all)
    upper_bound = peak_all / token_total + ridge_term
    center = (upper_bound + ridge_term) / 2.0
    half_span = (upper_bound - ridge_term) / 2.0
    ratio_now = half_span / center
    ratio_next = 1.0 / (2.0 * center / half_span - ratio_now)
    target = target_in[...]
    start = target / center
    residual = target - (applied + ridge_term * round_half(target)) / center
    update = ratio_next * ratio_now * start + 2.0 * ratio_next / half_span * residual
    transform = start + update
    ratio_last = 1.0 / (2.0 * center / half_span - ratio_next)
    transform_out[...] = transform
    update_out[...] = update
    lane = lax.broadcasted_iota(jnp.int32, (8, 128), 1)
    scalars[...] = jnp.where(
        lane == 0,
        ridge_term,
        jnp.where(lane == 1, ratio_last * ratio_next, 2.0 * ratio_last / half_span),
    )
    half = transform.astype(jnp.bfloat16)
    for d in range(16):
        sent[d, :, : 2 * rows] = half
        sent[d, :, 2 * rows :] = jnp.zeros((40, 64), jnp.bfloat16)


def second_kernel(
    token_total, place, got, high, low, target_in, transform_in, update_in, scalars, out, seen
):
    quarter, half_cols = 40, 80
    applied = times_gram(place[1], got, high, low, seen) / token_total
    ridge_term, keep, gain = scalars[0:1, 0:1], scalars[0:1, 1:2], scalars[0:1, 2:3]
    transform = transform_in[...]
    residual = target_in[...] - (applied + ridge_term * round_half(transform))
    final = transform + (keep * update_in[...] + gain * residual)
    for g in range(4):
        out[quarter * g : quarter * (g + 1), :] = final[:, half_cols * g : half_cols * (g + 1)]


def body(entering, leaving):
    yl = lax.axis_index("yl")
    z = lax.axis_index("z")
    rows = entering.shape[0]
    quarter = rows // 4
    half_cols = rows // 2
    token_total = entering.shape[1] * 32
    order_all = rows * 16
    low = yl == 0

    first = [(z, (z + 1) % 8) for z in range(8)] + [(8 + z, 8 + z) for z in range(8)]
    later = [(z, (z + 1) % 8) for z in range(8)] + [(8 + z, 8 + (z + 7) % 8) for z in range(8)]
    swapped, entering, leaving = lax.optimization_barrier(
        (shift(entering, "c", 2, 1), entering, leaving)
    )
    chain = [lax.ppermute(jnp.stack([entering, swapped]), ("c", "z"), first)]
    pair = jnp.concatenate([entering, leaving], 0)
    other = shift(pair, "yl", 2, 1)
    chain.append(lax.ppermute(chain[0], ("c", "z"), later))
    chain[1], other = lax.optimization_barrier((chain[1], other))
    columns = jnp.concatenate(
        [
            jnp.where(low, pair[:rows], other[:rows]),
            jnp.where(low, other[:rows], pair[:rows]),
            jnp.where(low, pair[rows:], other[rows:]),
            jnp.where(low, other[rows:], pair[rows:]),
        ],
        0,
    )
    columns_there = shift(columns, "c", 2, 1)
    chain.append(lax.ppermute(chain[1], ("c", "z"), later))
    chain[2], columns_there = lax.optimization_barrier((chain[2], columns_there))
    chain.append(lax.ppermute(chain[2], ("c", "z"), later))
    partial = jnp.zeros((4, rows, 4 * rows), jnp.float32)
    for step in range(4):
        here, there = chain[step][0], chain[step][1]
        product = lax.dot_general(
            here, columns, (((1,), (1,)), ((), ())), preferred_element_type=jnp.float32
        ) + lax.dot_general(
            there, columns_there, (((1,), (1,)), ((), ())), preferred_element_type=jnp.float32
        )
        partial = lax.dynamic_update_index_in_dim(partial, product, step, 0)
    partial = jnp.sum(lax.all_to_all(partial, "x", 0, 0), 0)
    packed = []
    for to_yh in range(4):
        for to_yl in range(2):
            top = half_cols * to_yl
            left = 2 * rows + half_cols * to_yh
            packed.append(
                jnp.concatenate(
                    [
                        partial[
                            quarter * to_yh : quarter * (to_yh + 1),
                            rows * to_yl : rows * (to_yl + 1),
                        ],
                        partial[top : top + quarter, left : left + half_cols],
                        partial[top + quarter : top + 2 * quarter, left : left + half_cols],
                    ],
                    1,
                )
            )
    own = lax.all_to_all(jnp.stack(packed), ("yh", "yl"), 0, 0)
    own = jnp.sum(own.reshape(4, 2, quarter, 2 * rows), 0)

    cross_own = jnp.concatenate([own[0, :, rows:], own[1, :, rows:]], 1)
    cross_own = lax.ppermute(cross_own, ALL, tile_moves())
    cross_swap = shift(cross_own, "yl", 2, 1)
    target = jnp.where(
        low,
        jnp.concatenate([cross_own[:, :rows], cross_swap[:, :rows]], 1),
        jnp.concatenate([cross_swap[:, rows:], cross_own[:, rows:]], 1),
    ) / token_total

    gram_part = jnp.concatenate([own[0, :, :rows], own[1, :, :rows]], 1)
    gram_part = spread(gram_part, "yh", 4)
    gram_part = jnp.concatenate([gram_part[q] for q in range(4)], 1)
    gram_part = spread(gram_part, "x", 4)
    gram = spread(gram_part, "c", 2).reshape(8, quarter, 8 * rows)

    place = jnp.stack([yl, z]).astype(jnp.int32)
    vmem = pl.BlockSpec(memory_space=pltpu.VMEM)
    smem = pl.BlockSpec(memory_space=pltpu.SMEM)
    params = pltpu.CompilerParams(vmem_limit_bytes=40 * 2**20)
    tile = jax.ShapeDtypeStruct((quarter, 2 * rows), jnp.float32)
    message = jax.ShapeDtypeStruct((16, quarter, 2 * rows + 64), jnp.bfloat16)
    half_gram = jax.ShapeDtypeStruct((16 * rows, rows), jnp.bfloat16)
    columns_seen = pltpu.VMEM((16 * rows, half_cols), jnp.float32)
    gram_high, gram_low, sent = pl.pallas_call(
        split_kernel,
        out_shape=(half_gram, half_gram, message),
        in_specs=[smem, vmem, vmem],
        out_specs=(vmem, vmem, vmem),
        compiler_params=params,
    )(place, gram, target)
    got = lax.all_to_all(sent, FEAT, 0, 0)
    transform, update, sent, scalars = pl.pallas_call(
        functools.partial(first_kernel, token_total, order_all),
        out_shape=(tile, tile, message, jax.ShapeDtypeStruct((8, 128), jnp.float32)),
        in_specs=[smem] + [vmem] * 4,
        out_specs=(vmem,) * 4,
        scratch_shapes=[columns_seen],
        compiler_params=params,
    )(place, got, gram_high, gram_low, target)
    got = lax.all_to_all(sent, FEAT, 0, 0)
    return pl.pallas_call(
        functools.partial(second_kernel, token_total),
        out_shape=jax.ShapeDtypeStruct((rows, half_cols), jnp.float32),
        in_specs=[smem] + [vmem] * 7,
        out_specs=vmem,
        scratch_shapes=[columns_seen],
        compiler_params=params,
    )(place, got, gram_high, gram_low, target, transform, update, scalars)


def solution(mesh):
    fine = Mesh(mesh.devices.reshape(SIZES), ALL)
    spec = P(FEAT, TOK)
    return jax.shard_map(
        body, mesh=fine, in_specs=(spec, spec), out_specs=spec, check_vma=False
    )
```

```python
import functools

import jax
import jax.numpy as jnp
from jax import lax
from jax.experimental import pallas as pl
from jax.experimental.pallas import tpu as pltpu
from jax.sharding import Mesh, PartitionSpec as P

ITERS = 2
ridge_share = 0.2
TOK = ("yh", "x", "c")
FEAT = ("yl", "z")
ALL = TOK + FEAT
SIZES = (4, 4, 2, 2, 8)
OFFSETS = (7, 6, 5, 4, 0, 1, 2, 3)


def shift(array, axis, size, step):
    return lax.ppermute(array, axis, [(i, (i + step) % size) for i in range(size)])


def spread(array, axes, count):
    return lax.all_to_all(
        jnp.broadcast_to(array[None], (count,) + array.shape), axes, 0, 0
    )


def tile_moves():
    moves = []
    for yh in range(4):
        for x in range(4):
            for c in range(2):
                for yl in range(2):
                    for z in range(8):
                        other_yl, half = yh // 2, yh % 2
                        source = (((yh * 4 + x) * 2 + c) * 2 + yl) * 8 + z
                        to_z = (z + OFFSETS[4 * c + x]) % 8
                        to_yh, to_x = other_yl * 2 + z // 4, z % 4
                        target = (((to_yh * 4 + to_x) * 2 + half) * 2 + yl) * 8 + to_z
                        moves.append((source, target))
    return moves


def round_half(array):
    return array.astype(jnp.bfloat16).astype(jnp.float32)


def split_kernel(place, gram, target, high_out, low_out, sent):
    yl = place[0]
    rows, quarter = 160, 40
    sums = jnp.zeros((1, rows), jnp.float32)
    trace = jnp.zeros((1, 1), jnp.float32)
    at_row = lax.broadcasted_iota(jnp.int32, (quarter, rows), 0)
    at_col = lax.broadcasted_iota(jnp.int32, (quarter, rows), 1)
    for q in range(4):
        for k in range(2):
            n = q * 2 + k
            block = gram[:, :, n * rows : (n + 1) * rows].reshape(2 * rows, rows)
            sums += jnp.sum(jnp.abs(block), 0, keepdims=True)
            on_diagonal = (at_col == at_row + quarter * q) & (yl == k)
            own = block[4 * quarter : 5 * quarter]
            trace += jnp.sum(jnp.where(on_diagonal, own, 0.0), keepdims=True)
            high = block.astype(jnp.bfloat16)
            high_out[n * 2 * rows : (n + 1) * 2 * rows, :] = high
            low_out[n * 2 * rows : (n + 1) * 2 * rows, :] = (
                block - high.astype(jnp.float32)
            ).astype(jnp.bfloat16)
    peak = jnp.max(sums, keepdims=True)
    lane = lax.broadcasted_iota(jnp.int32, (quarter, 64), 1)
    value = jnp.where(lane < 3, peak, trace)
    first = round_half(value)
    second = round_half(value - first)
    third = value - first - second
    which = lane % 3
    tail = jnp.where(which == 0, first, jnp.where(which == 1, second, third))
    body_half = target[...].astype(jnp.bfloat16)
    tail_half = tail.astype(jnp.bfloat16)
    for d in range(16):
        sent[d, :, : 2 * rows] = body_half
        sent[d, :, 2 * rows :] = tail_half


def times_gram(z, got, high, low, seen):
    rows, quarter, half_cols = 160, 40, 80
    for k in range(2):
        for s in range(8):
            block = got[8 * k + lax.rem(z + OFFSETS[s], 8)].astype(jnp.float32)
            for q in range(4):
                top = (q * 2 + k) * 2 * rows + s * quarter
                seen[top : top + quarter, :] = block[:, q * half_cols : (q + 1) * half_cols]
    side = seen[...].astype(jnp.bfloat16)
    product = 0.0
    for part in (high, low):
        product += lax.dot_general(
            part[...], side, (((0,), (0,)), ((), ())), preferred_element_type=jnp.float32
        )
    return jnp.concatenate([product[quarter * g : quarter * (g + 1)] for g in range(4)], 1)


def first_kernel(
    token_total, order_all, place, got, high, low, target_in, transform_out, update_out,
    sent, scalars, seen,
):
    rows = 160
    applied = times_gram(place[1], got, high, low, seen) / token_total
    peak_all = energy = None
    for d in range(16):
        tail = got[d][:, 2 * rows :].astype(jnp.float32)[:1]
        peak = tail[:, 0:1] + tail[:, 1:2] + tail[:, 2:3]
        trace = tail[:, 3:4] + tail[:, 4:5] + tail[:, 5:6]
        peak_all = peak if d == 0 else jnp.maximum(peak_all, peak)
        energy = trace if d == 0 else energy + trace
    ridge_term = ridge_share * energy / (token_total * order_all)
    upper_bound = peak_all / token_total + ridge_term
    center = (upper_bound + ridge_term) / 2.0
    half_span = (upper_bound - ridge_term) / 2.0
    ratio_now = half_span / center
    ratio_next = 1.0 / (2.0 * center / half_span - ratio_now)
    target = target_in[...]
    start = target / center
    residual = target - (applied + ridge_term * round_half(target)) / center
    update = ratio_next * ratio_now * start + 2.0 * ratio_next / half_span * residual
    transform = start + update
    ratio_last = 1.0 / (2.0 * center / half_span - ratio_next)
    transform_out[...] = transform
    update_out[...] = update
    lane = lax.broadcasted_iota(jnp.int32, (8, 128), 1)
    scalars[...] = jnp.where(
        lane == 0,
        ridge_term,
        jnp.where(lane == 1, ratio_last * ratio_next, 2.0 * ratio_last / half_span),
    )
    half = transform.astype(jnp.bfloat16)
    for d in range(16):
        sent[d, :, : 2 * rows] = half
        sent[d, :, 2 * rows :] = jnp.zeros((40, 64), jnp.bfloat16)


def second_kernel(
    token_total, place, got, high, low, target_in, transform_in, update_in, scalars, out, seen
):
    quarter, half_cols = 40, 80
    applied = times_gram(place[1], got, high, low, seen) / token_total
    ridge_term, keep, gain = scalars[0:1, 0:1], scalars[0:1, 1:2], scalars[0:1, 2:3]
    transform = transform_in[...]
    residual = target_in[...] - (applied + ridge_term * round_half(transform))
    final = transform + (keep * update_in[...] + gain * residual)
    for g in range(4):
        out[quarter * g : quarter * (g + 1), :] = final[:, half_cols * g : half_cols * (g + 1)]


def body(entering, leaving):
    yl = lax.axis_index("yl")
    z = lax.axis_index("z")
    rows = entering.shape[0]
    quarter = rows // 4
    half_cols = rows // 2
    token_total = entering.shape[1] * 32
    order_all = rows * 16
    low = yl == 0

    first = [(z, (z + 1) % 8) for z in range(8)] + [(8 + z, 8 + z) for z in range(8)]
    later = [(z, (z + 1) % 8) for z in range(8)] + [(8 + z, 8 + (z + 7) % 8) for z in range(8)]
    here, there = [lax.ppermute(entering, ("c", "z"), first)], []
    swapped, entering, leaving = lax.optimization_barrier(
        (shift(entering, "c", 2, 1), entering, leaving)
    )
    there.append(lax.ppermute(swapped, ("c", "z"), first))
    pair = jnp.concatenate([entering, leaving], 0)
    other = shift(pair, "yl", 2, 1)
    here[0], there[0] = lax.optimization_barrier((here[0], there[0]))
    here.append(lax.ppermute(here[0], ("c", "z"), later))
    there.append(lax.ppermute(there[0], ("c", "z"), later))
    here[1], there[1], other = lax.optimization_barrier((here[1], there[1], other))
    columns = jnp.concatenate(
        [
            jnp.where(low, pair[:rows], other[:rows]),
            jnp.where(low, other[:rows], pair[:rows]),
            jnp.where(low, pair[rows:], other[rows:]),
            jnp.where(low, other[rows:], pair[rows:]),
        ],
        0,
    )
    columns_there = shift(columns, "c", 2, 1)
    here.append(lax.ppermute(here[1], ("c", "z"), later))
    there.append(lax.ppermute(there[1], ("c", "z"), later))
    here[2], columns_there = lax.optimization_barrier((here[2], columns_there))
    here.append(lax.ppermute(here[2], ("c", "z"), later))
    there.append(lax.ppermute(there[2], ("c", "z"), later))
    partial = jnp.zeros((4, rows, 4 * rows), jnp.float32)
    for step in range(4):
        product = lax.dot_general(
            here[step], columns, (((1,), (1,)), ((), ())), preferred_element_type=jnp.float32
        ) + lax.dot_general(
            there[step], columns_there, (((1,), (1,)), ((), ())), preferred_element_type=jnp.float32
        )
        partial = lax.dynamic_update_index_in_dim(partial, product, step, 0)
    partial = jnp.sum(lax.all_to_all(partial, "x", 0, 0), 0)
    packed = []
    for to_yh in range(4):
        for to_yl in range(2):
            top = half_cols * to_yl
            left = 2 * rows + half_cols * to_yh
            packed.append(
                jnp.concatenate(
                    [
                        partial[
                            quarter * to_yh : quarter * (to_yh + 1),
                            rows * to_yl : rows * (to_yl + 1),
                        ],
                        partial[top : top + quarter, left : left + half_cols],
                        partial[top + quarter : top + 2 * quarter, left : left + half_cols],
                    ],
                    1,
                )
            )
    own = lax.all_to_all(jnp.stack(packed), ("yh", "yl"), 0, 0)
    own = jnp.sum(own.reshape(4, 2, quarter, 2 * rows), 0)

    cross_own = jnp.concatenate([own[0, :, rows:], own[1, :, rows:]], 1)
    cross_own = lax.ppermute(cross_own, ALL, tile_moves())
    cross_swap = shift(cross_own, "yl", 2, 1)
    target = jnp.where(
        low,
        jnp.concatenate([cross_own[:, :rows], cross_swap[:, :rows]], 1),
        jnp.concatenate([cross_swap[:, rows:], cross_own[:, rows:]], 1),
    ) / token_total

    gram_part = jnp.concatenate([own[0, :, :rows], own[1, :, :rows]], 1)
    gram_part = spread(gram_part, "yh", 4)
    gram_part = jnp.concatenate([gram_part[q] for q in range(4)], 1)
    gram_part = spread(gram_part, "x", 4)
    gram = spread(gram_part, "c", 2).reshape(8, quarter, 8 * rows)

    place = jnp.stack([yl, z]).astype(jnp.int32)
    vmem = pl.BlockSpec(memory_space=pltpu.VMEM)
    smem = pl.BlockSpec(memory_space=pltpu.SMEM)
    params = pltpu.CompilerParams(vmem_limit_bytes=40 * 2**20)
    tile = jax.ShapeDtypeStruct((quarter, 2 * rows), jnp.float32)
    message = jax.ShapeDtypeStruct((16, quarter, 2 * rows + 64), jnp.bfloat16)
    half_gram = jax.ShapeDtypeStruct((16 * rows, rows), jnp.bfloat16)
    columns_seen = pltpu.VMEM((16 * rows, half_cols), jnp.float32)
    gram_high, gram_low, sent = pl.pallas_call(
        split_kernel,
        out_shape=(half_gram, half_gram, message),
        in_specs=[smem, vmem, vmem],
        out_specs=(vmem, vmem, vmem),
        compiler_params=params,
    )(place, gram, target)
    got = lax.all_to_all(sent, FEAT, 0, 0)
    transform, update, sent, scalars = pl.pallas_call(
        functools.partial(first_kernel, token_total, order_all),
        out_shape=(tile, tile, message, jax.ShapeDtypeStruct((8, 128), jnp.float32)),
        in_specs=[smem] + [vmem] * 4,
        out_specs=(vmem,) * 4,
        scratch_shapes=[columns_seen],
        compiler_params=params,
    )(place, got, gram_high, gram_low, target)
    got = lax.all_to_all(sent, FEAT, 0, 0)
    return pl.pallas_call(
        functools.partial(second_kernel, token_total),
        out_shape=jax.ShapeDtypeStruct((rows, half_cols), jnp.float32),
        in_specs=[smem] + [vmem] * 7,
        out_specs=vmem,
        scratch_shapes=[columns_seen],
        compiler_params=params,
    )(place, got, gram_high, gram_low, target, transform, update, scalars)


def solution(mesh):
    fine = Mesh(mesh.devices.reshape(SIZES), ALL)
    spec = P(FEAT, TOK)
    return jax.shard_map(
        body, mesh=fine, in_specs=(spec, spec), out_specs=spec, check_vma=False
    )
```

```python
import functools

import jax
import jax.numpy as jnp
from jax import lax
from jax.experimental import pallas as pl
from jax.experimental.pallas import tpu as pltpu
from jax.sharding import Mesh, PartitionSpec as P

ITERS = 2
ridge_share = 0.2
TOK = ("yh", "x", "c")
FEAT = ("yl", "z")
ALL = TOK + FEAT
SIZES = (4, 4, 2, 2, 8)
OFFSETS = (7, 6, 5, 4, 0, 1, 2, 3)


def shift(array, axis, size, step):
    return lax.ppermute(array, axis, [(i, (i + step) % size) for i in range(size)])


def spread(array, axes, count):
    return lax.all_to_all(
        jnp.broadcast_to(array[None], (count,) + array.shape), axes, 0, 0
    )


def tile_moves():
    moves = []
    for yh in range(4):
        for x in range(4):
            for c in range(2):
                for yl in range(2):
                    for z in range(8):
                        other_yl, half = yh // 2, yh % 2
                        source = (((yh * 4 + x) * 2 + c) * 2 + yl) * 8 + z
                        to_z = (z + OFFSETS[4 * c + x]) % 8
                        to_yh, to_x = other_yl * 2 + z // 4, z % 4
                        target = (((to_yh * 4 + to_x) * 2 + half) * 2 + yl) * 8 + to_z
                        moves.append((source, target))
    return moves


def round_half(array):
    return array.astype(jnp.bfloat16).astype(jnp.float32)


def split_kernel(place, gram, target, high_out, low_out, sent):
    yl = place[0]
    rows, quarter = 160, 40
    sums = jnp.zeros((1, rows), jnp.float32)
    trace = jnp.zeros((1, 1), jnp.float32)
    at_row = lax.broadcasted_iota(jnp.int32, (quarter, rows), 0)
    at_col = lax.broadcasted_iota(jnp.int32, (quarter, rows), 1)
    for q in range(4):
        for k in range(2):
            n = q * 2 + k
            block = gram[:, :, n * rows : (n + 1) * rows].reshape(2 * rows, rows)
            sums += jnp.sum(jnp.abs(block), 0, keepdims=True)
            on_diagonal = (at_col == at_row + quarter * q) & (yl == k)
            own = block[4 * quarter : 5 * quarter]
            trace += jnp.sum(jnp.where(on_diagonal, own, 0.0), keepdims=True)
            high = block.astype(jnp.bfloat16)
            high_out[n * 2 * rows : (n + 1) * 2 * rows, :] = high
            low_out[n * 2 * rows : (n + 1) * 2 * rows, :] = (
                block - high.astype(jnp.float32)
            ).astype(jnp.bfloat16)
    peak = jnp.max(sums, keepdims=True)
    lane = lax.broadcasted_iota(jnp.int32, (quarter, 64), 1)
    value = jnp.where(lane < 3, peak, trace)
    first = round_half(value)
    second = round_half(value - first)
    third = value - first - second
    which = lane % 3
    tail = jnp.where(which == 0, first, jnp.where(which == 1, second, third))
    body_half = target[...].astype(jnp.bfloat16)
    tail_half = tail.astype(jnp.bfloat16)
    for d in range(16):
        sent[d, :, : 2 * rows] = body_half
        sent[d, :, 2 * rows :] = tail_half


def times_gram(z, got, high, low, seen):
    rows, quarter, half_cols = 160, 40, 80
    for k in range(2):
        for s in range(8):
            block = got[8 * k + lax.rem(z + OFFSETS[s], 8)].astype(jnp.float32)
            for q in range(4):
                top = (q * 2 + k) * 2 * rows + s * quarter
                seen[top : top + quarter, :] = block[:, q * half_cols : (q + 1) * half_cols]
    side = seen[...].astype(jnp.bfloat16)
    product = 0.0
    for part in (high, low):
        product += lax.dot_general(
            part[...], side, (((0,), (0,)), ((), ())), preferred_element_type=jnp.float32
        )
    return jnp.concatenate([product[quarter * g : quarter * (g + 1)] for g in range(4)], 1)


def first_kernel(
    token_total, order_all, place, got, high, low, target_in, transform_out, update_out,
    sent, scalars, seen,
):
    rows = 160
    applied = times_gram(place[1], got, high, low, seen) / token_total
    peak_all = energy = None
    for d in range(16):
        tail = got[d][:, 2 * rows :].astype(jnp.float32)[:1]
        peak = tail[:, 0:1] + tail[:, 1:2] + tail[:, 2:3]
        trace = tail[:, 3:4] + tail[:, 4:5] + tail[:, 5:6]
        peak_all = peak if d == 0 else jnp.maximum(peak_all, peak)
        energy = trace if d == 0 else energy + trace
    ridge_term = ridge_share * energy / (token_total * order_all)
    upper_bound = peak_all / token_total + ridge_term
    center = (upper_bound + ridge_term) / 2.0
    half_span = (upper_bound - ridge_term) / 2.0
    ratio_now = half_span / center
    ratio_next = 1.0 / (2.0 * center / half_span - ratio_now)
    target = target_in[...]
    start = target / center
    residual = target - (applied + ridge_term * round_half(target)) / center
    update = ratio_next * ratio_now * start + 2.0 * ratio_next / half_span * residual
    transform = start + update
    ratio_last = 1.0 / (2.0 * center / half_span - ratio_next)
    transform_out[...] = transform
    update_out[...] = update
    lane = lax.broadcasted_iota(jnp.int32, (8, 128), 1)
    scalars[...] = jnp.where(
        lane == 0,
        ridge_term,
        jnp.where(lane == 1, ratio_last * ratio_next, 2.0 * ratio_last / half_span),
    )
    half = transform.astype(jnp.bfloat16)
    for d in range(16):
        sent[d, :, : 2 * rows] = half
        sent[d, :, 2 * rows :] = jnp.zeros((40, 64), jnp.bfloat16)


def second_kernel(
    token_total, place, got, high, low, target_in, transform_in, update_in, scalars, out, seen
):
    quarter, half_cols = 40, 80
    applied = times_gram(place[1], got, high, low, seen) / token_total
    ridge_term, keep, gain = scalars[0:1, 0:1], scalars[0:1, 1:2], scalars[0:1, 2:3]
    transform = transform_in[...]
    residual = target_in[...] - (applied + ridge_term * round_half(transform))
    final = transform + (keep * update_in[...] + gain * residual)
    for g in range(4):
        out[quarter * g : quarter * (g + 1), :] = final[:, half_cols * g : half_cols * (g + 1)]


def body(entering, leaving):
    yl = lax.axis_index("yl")
    z = lax.axis_index("z")
    rows = entering.shape[0]
    quarter = rows // 4
    half_cols = rows // 2
    token_total = entering.shape[1] * 32
    order_all = rows * 16
    low = yl == 0

    first = [(z, (z + 1) % 8) for z in range(8)] + [(8 + z, 8 + z) for z in range(8)]
    later = [(z, (z + 1) % 8) for z in range(8)] + [(8 + z, 8 + (z + 7) % 8) for z in range(8)]
    here, there = [lax.ppermute(entering, ("c", "z"), first)], []
    swapped, entering, leaving = lax.optimization_barrier(
        (shift(entering, "c", 2, 1), entering, leaving)
    )
    there.append(lax.ppermute(swapped, ("c", "z"), first))
    pair = jnp.concatenate([entering, leaving], 0)
    other = shift(pair, "yl", 2, 1)
    here.append(lax.ppermute(here[0], ("c", "z"), later))
    there.append(lax.ppermute(there[0], ("c", "z"), later))
    here[1], there[1], other = lax.optimization_barrier((here[1], there[1], other))
    columns = jnp.concatenate(
        [
            jnp.where(low, pair[:rows], other[:rows]),
            jnp.where(low, other[:rows], pair[:rows]),
            jnp.where(low, pair[rows:], other[rows:]),
            jnp.where(low, other[rows:], pair[rows:]),
        ],
        0,
    )
    columns_there = shift(columns, "c", 2, 1)
    here.append(lax.ppermute(here[1], ("c", "z"), later))
    there.append(lax.ppermute(there[1], ("c", "z"), later))
    here[2], columns_there = lax.optimization_barrier((here[2], columns_there))
    here.append(lax.ppermute(here[2], ("c", "z"), later))
    there.append(lax.ppermute(there[2], ("c", "z"), later))
    partial = jnp.zeros((4, rows, 4 * rows), jnp.float32)
    for step in range(4):
        product = lax.dot_general(
            here[step], columns, (((1,), (1,)), ((), ())), preferred_element_type=jnp.float32
        ) + lax.dot_general(
            there[step], columns_there, (((1,), (1,)), ((), ())), preferred_element_type=jnp.float32
        )
        partial = lax.dynamic_update_index_in_dim(partial, product, step, 0)
    partial = jnp.sum(lax.all_to_all(partial, "x", 0, 0), 0)
    packed = []
    for to_yh in range(4):
        for to_yl in range(2):
            top = half_cols * to_yl
            left = 2 * rows + half_cols * to_yh
            packed.append(
                jnp.concatenate(
                    [
                        partial[
                            quarter * to_yh : quarter * (to_yh + 1),
                            rows * to_yl : rows * (to_yl + 1),
                        ],
                        partial[top : top + quarter, left : left + half_cols],
                        partial[top + quarter : top + 2 * quarter, left : left + half_cols],
                    ],
                    1,
                )
            )
    own = lax.all_to_all(jnp.stack(packed), ("yh", "yl"), 0, 0)
    own = jnp.sum(own.reshape(4, 2, quarter, 2 * rows), 0)

    cross_own = jnp.concatenate([own[0, :, rows:], own[1, :, rows:]], 1)
    cross_own = lax.ppermute(cross_own, ALL, tile_moves())
    cross_swap = shift(cross_own, "yl", 2, 1)
    target = jnp.where(
        low,
        jnp.concatenate([cross_own[:, :rows], cross_swap[:, :rows]], 1),
        jnp.concatenate([cross_swap[:, rows:], cross_own[:, rows:]], 1),
    ) / token_total

    gram_part = jnp.concatenate([own[0, :, :rows], own[1, :, :rows]], 1)
    gram_part = spread(gram_part, "yh", 4)
    gram_part = jnp.concatenate([gram_part[q] for q in range(4)], 1)
    gram_part = spread(gram_part, "x", 4)
    gram = spread(gram_part, "c", 2).reshape(8, quarter, 8 * rows)

    place = jnp.stack([yl, z]).astype(jnp.int32)
    vmem = pl.BlockSpec(memory_space=pltpu.VMEM)
    smem = pl.BlockSpec(memory_space=pltpu.SMEM)
    params = pltpu.CompilerParams(vmem_limit_bytes=40 * 2**20)
    tile = jax.ShapeDtypeStruct((quarter, 2 * rows), jnp.float32)
    message = jax.ShapeDtypeStruct((16, quarter, 2 * rows + 64), jnp.bfloat16)
    half_gram = jax.ShapeDtypeStruct((16 * rows, rows), jnp.bfloat16)
    columns_seen = pltpu.VMEM((16 * rows, half_cols), jnp.float32)
    gram_high, gram_low, sent = pl.pallas_call(
        split_kernel,
        out_shape=(half_gram, half_gram, message),
        in_specs=[smem, vmem, vmem],
        out_specs=(vmem, vmem, vmem),
        compiler_params=params,
    )(place, gram, target)
    got = lax.all_to_all(sent, FEAT, 0, 0)
    transform, update, sent, scalars = pl.pallas_call(
        functools.partial(first_kernel, token_total, order_all),
        out_shape=(tile, tile, message, jax.ShapeDtypeStruct((8, 128), jnp.float32)),
        in_specs=[smem] + [vmem] * 4,
        out_specs=(vmem,) * 4,
        scratch_shapes=[columns_seen],
        compiler_params=params,
    )(place, got, gram_high, gram_low, target)
    got = lax.all_to_all(sent, FEAT, 0, 0)
    return pl.pallas_call(
        functools.partial(second_kernel, token_total),
        out_shape=jax.ShapeDtypeStruct((rows, half_cols), jnp.float32),
        in_specs=[smem] + [vmem] * 7,
        out_specs=vmem,
        scratch_shapes=[columns_seen],
        compiler_params=params,
    )(place, got, gram_high, gram_low, target, transform, update, scalars)


def solution(mesh):
    fine = Mesh(mesh.devices.reshape(SIZES), ALL)
    spec = P(FEAT, TOK)
    return jax.shard_map(
        body, mesh=fine, in_specs=(spec, spec), out_specs=spec, check_vma=False
    )
```

```python
import functools

import jax
import jax.numpy as jnp
from jax import lax
from jax.experimental import pallas as pl
from jax.experimental.pallas import tpu as pltpu
from jax.sharding import Mesh, PartitionSpec as P

ITERS = 2
ridge_share = 0.2
TOK = ("yh", "x", "c")
FEAT = ("yl", "z")
ALL = TOK + FEAT
SIZES = (4, 4, 2, 2, 8)
OFFSETS = (7, 6, 5, 4, 0, 1, 2, 3)


def shift(array, axis, size, step):
    return lax.ppermute(array, axis, [(i, (i + step) % size) for i in range(size)])


def spread(array, axes, count):
    return lax.all_to_all(
        jnp.broadcast_to(array[None], (count,) + array.shape), axes, 0, 0
    )


def tile_moves():
    moves = []
    for yh in range(4):
        for x in range(4):
            for c in range(2):
                for yl in range(2):
                    for z in range(8):
                        other_yl, half = yh // 2, yh % 2
                        source = (((yh * 4 + x) * 2 + c) * 2 + yl) * 8 + z
                        to_z = (z + OFFSETS[4 * c + x]) % 8
                        to_yh, to_x = other_yl * 2 + z // 4, z % 4
                        target = (((to_yh * 4 + to_x) * 2 + half) * 2 + yl) * 8 + to_z
                        moves.append((source, target))
    return moves


def round_half(array):
    return array.astype(jnp.bfloat16).astype(jnp.float32)


def split_kernel(place, gram, target, high_out, low_out, sent):
    yl = place[0]
    rows, quarter = 160, 40
    sums = jnp.zeros((1, rows), jnp.float32)
    trace = jnp.zeros((1, 1), jnp.float32)
    at_row = lax.broadcasted_iota(jnp.int32, (quarter, rows), 0)
    at_col = lax.broadcasted_iota(jnp.int32, (quarter, rows), 1)
    for q in range(4):
        for k in range(2):
            n = q * 2 + k
            block = gram[:, :, n * rows : (n + 1) * rows].reshape(2 * rows, rows)
            sums += jnp.sum(jnp.abs(block), 0, keepdims=True)
            on_diagonal = (at_col == at_row + quarter * q) & (yl == k)
            own = block[4 * quarter : 5 * quarter]
            trace += jnp.sum(jnp.where(on_diagonal, own, 0.0), keepdims=True)
            high = block.astype(jnp.bfloat16)
            high_out[n * 2 * rows : (n + 1) * 2 * rows, :] = high
            low_out[n * 2 * rows : (n + 1) * 2 * rows, :] = (
                block - high.astype(jnp.float32)
            ).astype(jnp.bfloat16)
    peak = jnp.max(sums, keepdims=True)
    lane = lax.broadcasted_iota(jnp.int32, (quarter, 64), 1)
    value = jnp.where(lane < 3, peak, trace)
    first = round_half(value)
    second = round_half(value - first)
    third = value - first - second
    which = lane % 3
    tail = jnp.where(which == 0, first, jnp.where(which == 1, second, third))
    body_half = target[...].astype(jnp.bfloat16)
    tail_half = tail.astype(jnp.bfloat16)
    for d in range(16):
        sent[d, :, : 2 * rows] = body_half
        sent[d, :, 2 * rows :] = tail_half


def times_gram(z, got, high, low, seen):
    rows, quarter, half_cols = 160, 40, 80
    for k in range(2):
        for s in range(8):
            block = got[8 * k + lax.rem(z + OFFSETS[s], 8)].astype(jnp.float32)
            for q in range(4):
                top = (q * 2 + k) * 2 * rows + s * quarter
                seen[top : top + quarter, :] = block[:, q * half_cols : (q + 1) * half_cols]
    side = seen[...].astype(jnp.bfloat16)
    product = 0.0
    for part in (high, low):
        product += lax.dot_general(
            part[...], side, (((0,), (0,)), ((), ())), preferred_element_type=jnp.float32
        )
    return jnp.concatenate([product[quarter * g : quarter * (g + 1)] for g in range(4)], 1)


def first_kernel(
    token_total, order_all, place, got, high, low, target_in, transform_out, update_out,
    sent, scalars, seen,
):
    rows = 160
    applied = times_gram(place[1], got, high, low, seen) / token_total
    peak_all = energy = None
    for d in range(16):
        tail = got[d][:, 2 * rows :].astype(jnp.float32)[:1]
        peak = tail[:, 0:1] + tail[:, 1:2] + tail[:, 2:3]
        trace = tail[:, 3:4] + tail[:, 4:5] + tail[:, 5:6]
        peak_all = peak if d == 0 else jnp.maximum(peak_all, peak)
        energy = trace if d == 0 else energy + trace
    ridge_term = ridge_share * energy / (token_total * order_all)
    upper_bound = peak_all / token_total + ridge_term
    center = (upper_bound + ridge_term) / 2.0
    half_span = (upper_bound - ridge_term) / 2.0
    ratio_now = half_span / center
    ratio_next = 1.0 / (2.0 * center / half_span - ratio_now)
    target = target_in[...]
    start = target / center
    residual = target - (applied + ridge_term * round_half(target)) / center
    update = ratio_next * ratio_now * start + 2.0 * ratio_next / half_span * residual
    transform = start + update
    ratio_last = 1.0 / (2.0 * center / half_span - ratio_next)
    transform_out[...] = transform
    update_out[...] = update
    lane = lax.broadcasted_iota(jnp.int32, (8, 128), 1)
    scalars[...] = jnp.where(
        lane == 0,
        ridge_term,
        jnp.where(lane == 1, ratio_last * ratio_next, 2.0 * ratio_last / half_span),
    )
    half = transform.astype(jnp.bfloat16)
    for d in range(16):
        sent[d, :, : 2 * rows] = half
        sent[d, :, 2 * rows :] = jnp.zeros((40, 64), jnp.bfloat16)


def second_kernel(
    token_total, place, got, high, low, target_in, transform_in, update_in, scalars, out, seen
):
    quarter, half_cols = 40, 80
    applied = times_gram(place[1], got, high, low, seen) / token_total
    ridge_term, keep, gain = scalars[0:1, 0:1], scalars[0:1, 1:2], scalars[0:1, 2:3]
    transform = transform_in[...]
    residual = target_in[...] - (applied + ridge_term * round_half(transform))
    final = transform + (keep * update_in[...] + gain * residual)
    for g in range(4):
        out[quarter * g : quarter * (g + 1), :] = final[:, half_cols * g : half_cols * (g + 1)]


def body(entering, leaving):
    yl = lax.axis_index("yl")
    z = lax.axis_index("z")
    rows = entering.shape[0]
    quarter = rows // 4
    half_cols = rows // 2
    token_total = entering.shape[1] * 32
    order_all = rows * 16
    low = yl == 0

    first = [(z, (z + 1) % 8) for z in range(8)] + [(8 + z, 8 + z) for z in range(8)]
    later = [(z, (z + 1) % 8) for z in range(8)] + [(8 + z, 8 + (z + 7) % 8) for z in range(8)]
    here, there = [lax.ppermute(entering, ("c", "z"), first)], []
    swapped, entering, leaving = lax.optimization_barrier(
        (shift(entering, "c", 2, 1), entering, leaving)
    )
    there.append(lax.ppermute(swapped, ("c", "z"), first))
    pair = jnp.concatenate([entering, leaving], 0)
    other = shift(pair, "yl", 2, 1)
    here.append(lax.ppermute(here[0], ("c", "z"), later))
    there.append(lax.ppermute(there[0], ("c", "z"), later))
    here[1], there[1], other = lax.optimization_barrier((here[1], there[1], other))
    columns = jnp.concatenate(
        [
            jnp.where(low, pair[:rows], other[:rows]),
            jnp.where(low, other[:rows], pair[:rows]),
            jnp.where(low, pair[rows:], other[rows:]),
            jnp.where(low, other[rows:], pair[rows:]),
        ],
        0,
    )
    columns_there = shift(columns, "c", 2, 1)
    here.append(lax.ppermute(here[1], ("c", "z"), later))
    there.append(lax.ppermute(there[1], ("c", "z"), later))
    there[2], columns_there = lax.optimization_barrier((there[2], columns_there))
    here.append(lax.ppermute(here[2], ("c", "z"), later))
    there.append(lax.ppermute(there[2], ("c", "z"), later))
    partial = jnp.zeros((4, rows, 4 * rows), jnp.float32)
    for step in range(4):
        product = lax.dot_general(
            here[step], columns, (((1,), (1,)), ((), ())), preferred_element_type=jnp.float32
        ) + lax.dot_general(
            there[step], columns_there, (((1,), (1,)), ((), ())), preferred_element_type=jnp.float32
        )
        partial = lax.dynamic_update_index_in_dim(partial, product, step, 0)
    partial = jnp.sum(lax.all_to_all(partial, "x", 0, 0), 0)
    packed = []
    for to_yh in range(4):
        for to_yl in range(2):
            top = half_cols * to_yl
            left = 2 * rows + half_cols * to_yh
            packed.append(
                jnp.concatenate(
                    [
                        partial[
                            quarter * to_yh : quarter * (to_yh + 1),
                            rows * to_yl : rows * (to_yl + 1),
                        ],
                        partial[top : top + quarter, left : left + half_cols],
                        partial[top + quarter : top + 2 * quarter, left : left + half_cols],
                    ],
                    1,
                )
            )
    own = lax.all_to_all(jnp.stack(packed), ("yh", "yl"), 0, 0)
    own = jnp.sum(own.reshape(4, 2, quarter, 2 * rows), 0)

    cross_own = jnp.concatenate([own[0, :, rows:], own[1, :, rows:]], 1)
    cross_own = lax.ppermute(cross_own, ALL, tile_moves())
    cross_swap = shift(cross_own, "yl", 2, 1)
    target = jnp.where(
        low,
        jnp.concatenate([cross_own[:, :rows], cross_swap[:, :rows]], 1),
        jnp.concatenate([cross_swap[:, rows:], cross_own[:, rows:]], 1),
    ) / token_total

    gram_part = jnp.concatenate([own[0, :, :rows], own[1, :, :rows]], 1)
    gram_part = spread(gram_part, "yh", 4)
    gram_part = jnp.concatenate([gram_part[q] for q in range(4)], 1)
    gram_part = spread(gram_part, "x", 4)
    gram = spread(gram_part, "c", 2).reshape(8, quarter, 8 * rows)

    place = jnp.stack([yl, z]).astype(jnp.int32)
    vmem = pl.BlockSpec(memory_space=pltpu.VMEM)
    smem = pl.BlockSpec(memory_space=pltpu.SMEM)
    params = pltpu.CompilerParams(vmem_limit_bytes=40 * 2**20)
    tile = jax.ShapeDtypeStruct((quarter, 2 * rows), jnp.float32)
    message = jax.ShapeDtypeStruct((16, quarter, 2 * rows + 64), jnp.bfloat16)
    half_gram = jax.ShapeDtypeStruct((16 * rows, rows), jnp.bfloat16)
    columns_seen = pltpu.VMEM((16 * rows, half_cols), jnp.float32)
    gram_high, gram_low, sent = pl.pallas_call(
        split_kernel,
        out_shape=(half_gram, half_gram, message),
        in_specs=[smem, vmem, vmem],
        out_specs=(vmem, vmem, vmem),
        compiler_params=params,
    )(place, gram, target)
    got = lax.all_to_all(sent, FEAT, 0, 0)
    transform, update, sent, scalars = pl.pallas_call(
        functools.partial(first_kernel, token_total, order_all),
        out_shape=(tile, tile, message, jax.ShapeDtypeStruct((8, 128), jnp.float32)),
        in_specs=[smem] + [vmem] * 4,
        out_specs=(vmem,) * 4,
        scratch_shapes=[columns_seen],
        compiler_params=params,
    )(place, got, gram_high, gram_low, target)
    got = lax.all_to_all(sent, FEAT, 0, 0)
    return pl.pallas_call(
        functools.partial(second_kernel, token_total),
        out_shape=jax.ShapeDtypeStruct((rows, half_cols), jnp.float32),
        in_specs=[smem] + [vmem] * 7,
        out_specs=vmem,
        scratch_shapes=[columns_seen],
        compiler_params=params,
    )(place, got, gram_high, gram_low, target, transform, update, scalars)


def solution(mesh):
    fine = Mesh(mesh.devices.reshape(SIZES), ALL)
    spec = P(FEAT, TOK)
    return jax.shard_map(
        body, mesh=fine, in_specs=(spec, spec), out_specs=spec, check_vma=False
    )
```
